128 devices in a mesh: dp: 16 (over z, y), tensor: 4 (over x), layer: 2 (over core).
Axes of the slice: x: 4, y: 4, z: 4, core: 2. Of those that a mesh axis runs over, the one named last changes fastest.
Arguments:
- hidden: bfloat16 [2, 16, 1024, 9216], P('layer', 'dp', None, 'tensor')
- out_grad: bfloat16 [2, 16, 1024, 2304], P('layer', 'dp', None, 'tensor'), may hold values from -6 to 6
- lengths: int32 [16], P('dp'), may hold values from 64 to 1024, as said below
- noise: float32 [2, 2304, 9216], P('layer', 'dp', 'tensor'), may hold values from -6 to 6
Outputs:
- noised_grad: bfloat16 [2, 2304, 9216], P('layer', None, 'tensor')
The draws below stay inside these ranges and needn't reach their ends.
Inputs may be any that keep to these rules, and one draw needn't show every extreme that they name: `lengths`: the first sequence is full and the second has 64 tokens.
All inputs are finite; a program needn't handle non-finite values.
Results may differ from the reference program's by a relative error of at most 0.019.
Values may be sent and summed in bfloat16 or wider, within the bound.
A program may use at most 192 MiB of HBM per device.

```python
import jax
import jax.numpy as jnp
from jax import lax

D = 2304
FF = 9216
LEN = 1024
SEQS = 16
LAYERS = 2
N_DP = 16


def draw_lengths(key, part):
    key = jax.random.fold_in(key, 7)
    shortest = max(1, LEN // 16)
    values = jax.random.randint(key, (SEQS,), shortest, LEN + 1).astype(jnp.int32)
    values = values.at[0].set(LEN)
    return values.at[1].set(shortest)


def draw_hidden(key, part):
    key = jax.random.fold_in(key, 11)
    column = jnp.arange(FF, dtype=jnp.float32) / FF
    level = jnp.arange(LAYERS, dtype=jnp.float32)
    base = jax.random.truncated_normal(key, -6.0, 6.0, (LAYERS, SEQS, LEN, FF), jnp.float32)
    rise = jnp.power(jnp.float32(3.0), column)
    layer_scale = jnp.power(jnp.float32(1.5), level)
    values = base * rise[None, None, None, :] * layer_scale[:, None, None, None]
    return values.astype(jnp.bfloat16)


def shard_levels(stream_key, dims, shards, least, top_value):
    factor_of, own = 1.0, jax.random.fold_in(stream_key, 6)
    for position, shards_of in shards:
        draws = jnp.exp(jax.random.uniform(jax.random.fold_in(own, position), (shards_of,), jnp.float32, least / len(shards), top_value / len(shards)))
        factor_of = factor_of * jnp.repeat(draws, dims[position] // shards_of).reshape([-1 if axis == position else 1 for axis in range(len(dims))])
    return factor_of


def gaussian(rng, dims, scale, reach, shards=(), kind=jnp.bfloat16):
    entries = scale * jax.random.normal(rng, dims, jnp.float32)
    if shards:
        entries = entries * shard_levels(rng, dims, shards, -0.22, 0.18)
    return jnp.clip(entries, -reach, reach).astype(kind)


def setup_inputs(seed: int = 0) -> dict:
    splits = jax.random.split(jax.random.key(seed), 5)
    hidden = draw_hidden(jax.random.fold_in(splits[4], 71), 0)
    out_grad = gaussian(splits[1], (LAYERS, SEQS, LEN, D), 1.0, 6.0, ((0, 2), (1, 16), (3, 4)))
    lengths = draw_lengths(jax.random.fold_in(splits[4], 71), 0)
    noise = gaussian(splits[3], (LAYERS, D, FF), 2.0, 6.0, ((0, 2), (1, 16), (2, 4)), jnp.float32)
    return dict(hidden=hidden, out_grad=out_grad, lengths=lengths, noise=noise)


def reference(hidden, out_grad, lengths, noise):
    layers, seqs, seq_len, units = hidden.shape
    width = out_grad.shape[3]
    bound = jnp.sqrt(jnp.float32(seq_len * layers * units * width / 64.0))
    seq_dev = seqs // N_DP
    positions = jnp.arange(seq_len, dtype=jnp.int32)

    def one_seq(index):
        valid = positions < lengths[index]
        grads = []
        for level in range(layers):
            kept = jnp.where(valid[:, None], hidden[level, index], jnp.zeros((), hidden.dtype))
            grads.append(jnp.dot(out_grad[level, index].T, kept, preferred_element_type=jnp.float32))
        stacked = jnp.stack(grads)
        squares = jnp.sum(stacked * stacked)
        factor = jnp.minimum(jnp.float32(1.0), bound / jnp.sqrt(squares + 1e-06))
        return factor * stacked

    def one_device(device):

        def add_seq(total, offset):
            return (total + one_seq(device * seq_dev + offset), None)
        start = jnp.zeros((layers, width, units), jnp.float32)
        total, _ = lax.scan(add_seq, start, jnp.arange(seq_dev, dtype=jnp.int32))
        return total.astype(jnp.bfloat16)

    def add_device(total, device):
        return (total + one_device(device).astype(jnp.float32), None)
    start = jnp.zeros((layers, width, units), jnp.float32)
    total, _ = lax.scan(add_device, start, jnp.arange(N_DP, dtype=jnp.int32))
    return ((total + noise) / seqs).astype(jnp.bfloat16)
```

```python
import functools

import jax
import jax.numpy as jnp
from jax import lax
from jax.experimental import pallas as pl
from jax.experimental.pallas import tpu as pltpu
from jax.sharding import PartitionSpec as P

MESH = pl.DeviceIdType.MESH
RING = 4
F32 = jnp.float32
BF16 = jnp.bfloat16


def kernel(bound, ot_hbm, h_hbm, noise_hbm, out_hbm,
           h_v, ot_v, g, r1, r2, fw, p1, p2, pf, nz, fin, sq, nrm, fac,
           load_sem, x_send, x_recv, raw_send, r1_recv, r2_recv, fw_send, fw_recv,
           p_send, p1_recv, p2_recv, pf_recv, nz_send, nz_recv, nrm_send, nrm_recv,
           fac_send, fac_recv, ag1_send, ag1_recv, ag2_send, ag2_recv, own_sem):
    dp = lax.axis_index("dp")
    x = lax.axis_index("tensor")
    core = lax.axis_index("layer")
    z, y = dp // RING, dp % RING
    block, tokens = ot_hbm.shape
    units = h_hbm.shape[1]
    piece = block // RING
    half = units // 2
    up = (piece // 32) * 16 + 16 * (piece // 16 % 2)
    down = piece - up

    def turn(i, by):
        return (i + by + RING) % RING

    z_up, z_down = {"dp": turn(z, 1) * RING + y}, {"dp": turn(z, -1) * RING + y}
    y_up, y_down = {"dp": z * RING + turn(y, 1)}, {"dp": z * RING + turn(y, -1)}
    x_up, x_down = {"tensor": turn(x, 1)}, {"tensor": turn(x, -1)}
    swap = {"dp": y * RING + z}
    q, r = (z, y), (y, z)
    q_up, q_down = (z_up, y_up), (z_down, y_down)
    r_up, r_down = (y_up, z_up), (y_down, z_down)
    cols = (pl.ds(0, half), pl.ds(half, half))

    def rows(b, p, start=0, size=None):
        return pl.ds(pl.multiple_of(b * block + p * piece + start, 16), piece if size is None else size)

    def remote(src, dst, send, recv, device):
        pltpu.make_async_remote_copy(src_ref=src, dst_ref=dst, send_sem=send, recv_sem=recv,
                                     device_id=device, device_id_type=MESH).start()

    def await_bytes(ref, sem):
        pltpu.make_async_copy(ref, ref, sem).wait()

    me = x * 2 + core
    group = []
    for k in range(1, 2 * RING):
        other = (me + k) % (2 * RING)
        group.append({"tensor": other // 2, "layer": other % 2})

    load_h = pltpu.make_async_copy(h_hbm, h_v, load_sem.at[0])
    load_h.start()
    load_o = pltpu.make_async_copy(ot_hbm, ot_v.at[pl.ds(pl.multiple_of(x * block, 16), block)], load_sem.at[1])
    load_o.start()
    load_n = pltpu.make_async_copy(noise_hbm.at[:, cols[1]], nz.at[1], load_sem.at[2])
    load_n.start()

    barrier = pltpu.get_barrier_semaphore()
    for device in group + [z_up, z_down, y_up, y_down]:
        pl.semaphore_signal(barrier, inc=1, device_id=device, device_id_type=MESH)

    @pl.when(z != y)
    def _():
        pl.semaphore_signal(barrier, inc=1, device_id=swap, device_id_type=MESH)
        pl.semaphore_wait(barrier, 12)

    @pl.when(z == y)
    def _():
        pl.semaphore_wait(barrier, 11)

    load_o.wait()

    def x_start(m):
        own = m < RING
        b, p = jnp.where(own, x, turn(x, -1)), jnp.where(own, m, m - 4)
        at = ot_v.at[rows(b, p)]
        remote(at, at, x_send.at[0, m], x_recv.at[0, m], x_up)
        b, p = jnp.where(own, x, turn(x, 1)), jnp.where(own, m, m - 2)
        at = ot_v.at[rows(b, p)]
        remote(at, at, x_send.at[1, m], x_recv.at[1, m], x_down)

    x_start(jnp.int32(0))
    x_start(jnp.int32(1))

    @pl.when(z != y)
    def _():
        remote(noise_hbm.at[:, cols[0]], nz.at[0], nz_send, nz_recv, swap)

    @pl.when(z == y)
    def _():
        pltpu.make_async_copy(noise_hbm.at[:, cols[0]], nz.at[0], nz_recv).start()

    sq[...] = jnp.zeros_like(sq)
    load_h.wait()

    def product(ba, pa, bb, pb):
        wide = sq.shape[1]

        @pl.loop(0, units // wide)
        def _(n):
            at = pl.ds(pl.multiple_of(n * wide, wide), wide)
            left = jnp.concatenate([ot_v[rows(ba, pa)], ot_v[rows(bb, pb)]], axis=0)
            out = jnp.dot(left, h_v[:, at], preferred_element_type=F32)
            sq[...] += jnp.sum((out * out).reshape(2 * piece // 8, 8, wide), axis=0)
            low = out.astype(BF16)
            g[rows(ba, pa), at] = low[:piece]
            g[rows(bb, pb), at] = low[piece:]

    def send_raw(b, p):
        for h in range(2):
            away = turn(p - q[h], 0)
            upper = g.at[rows(b, p, 0, up), cols[h]]
            lower = g.at[rows(b, p, up, down), cols[h]]

            @pl.when(away == 1)
            def _():
                remote(lower, r2.at[h, b, pl.ds(up, down)], raw_send.at[h, b], r2_recv.at[h, b], q_up[h])

            @pl.when(away == 2)
            def _():
                remote(upper, r1.at[h, b, pl.ds(0, up)], raw_send.at[h, b], r1_recv.at[h, b], q_up[h])
                remote(lower, r1.at[h, b, pl.ds(up, down)], raw_send.at[h, b], r1_recv.at[h, b], q_down[h])

            @pl.when(away == 3)
            def _():
                remote(upper, r2.at[h, b, pl.ds(0, up)], raw_send.at[h, b], r2_recv.at[h, b], q_down[h])

    @pl.loop(0, 2)
    def _(i):
        product(x, 2 * i, x, 2 * i + 1)
        send_raw(x, 2 * i)
        send_raw(x, 2 * i + 1)

    @pl.loop(0, 6)
    def _(i):
        near = i < RING
        ba, pa = jnp.where(near, turn(x, -1), turn(x, 2)), jnp.where(near, i, i - 4)
        bb, pb = jnp.where(near, turn(x, 1), turn(x, 2)), jnp.where(near, i, i - 2)
        await_bytes(ot_v.at[rows(ba, pa)], x_recv.at[0, i])
        await_bytes(ot_v.at[rows(bb, pb)], x_recv.at[1, i])

        @pl.when(i < 4)
        def _():
            await_bytes(ot_v.at[pl.ds(0, piece)], x_send.at[0, i])
            await_bytes(ot_v.at[pl.ds(0, piece)], x_send.at[1, i])
            x_start(i + 2)

        product(ba, pa, bb, pb)
        send_raw(ba, pa)
        send_raw(bb, pb)

    nrm[pl.ds(me, 1)] = (sq[:, :128] + sq[:, 128:])[None]
    for device in group:
        remote(nrm.at[me], nrm.at[me], nrm_send, nrm_recv, device)
    await_bytes(nrm.at[pl.ds(0, 7)], nrm_recv)
    total = jnp.sum(jnp.sum(nrm[...], axis=0), keepdims=True)
    factor = jnp.minimum(jnp.float32(1.0), bound / jnp.sqrt(total + 1e-06))
    fac[0] = jnp.broadcast_to(factor, fac.shape[1:])
    for slot, device in ((1, z_up), (2, z_down), (3, y_up), (4, y_down)):
        remote(fac.at[0], fac.at[slot], fac_send, fac_recv, device)
    await_bytes(fac.at[pl.ds(1, 4)], fac_recv)
    scale = fac[0, 0:1, 0:1]
    before = (fac[1, 0:1, 0:1], fac[3, 0:1, 0:1])
    after = (fac[2, 0:1, 0:1], fac[4, 0:1, 0:1])

    def strips(size, body):
        @pl.loop(0, size // 16)
        def _(n):
            body(pl.multiple_of(n * 16, 16))

    def away_of(i):
        return jnp.where(i == 0, 2, jnp.where(i == 1, 1, jnp.where(i == 2, 3, 0)))

    @pl.loop(0, RING)
    def _(i):
        for h in range(2):
            b = turn(r[h], away_of(i))
            await_bytes(r1.at[h, b], r1_recv.at[h, b])

            def upper(n):
                at = rows(b, turn(q[h], 1), n, 16)
                g[at, cols[h]] = (scale * g[at, cols[h]].astype(F32)
                                  + before[h] * r1[h, b, pl.ds(n, 16)].astype(F32)).astype(BF16)

            strips(up, upper)
            remote(g.at[rows(b, turn(q[h], 1), 0, up), cols[h]], fw.at[h, b, pl.ds(0, up)],
                   fw_send.at[h, b], fw_recv.at[h, b], q_up[h])

            def lower(n):
                at = rows(b, turn(q[h], -1), up + n, 16)
                g[at, cols[h]] = (scale * g[at, cols[h]].astype(F32)
                                  + after[h] * r1[h, b, pl.ds(up + n, 16)].astype(F32)).astype(BF16)

            strips(down, lower)
            remote(g.at[rows(b, turn(q[h], -1), up, down), cols[h]], fw.at[h, b, pl.ds(up, down)],
                   fw_send.at[h, b], fw_recv.at[h, b], q_down[h])

    @pl.loop(0, RING)
    def _(i):
        away = away_of(i)
        for h in range(2):
            b = turn(r[h], away)
            await_bytes(r2.at[h, b], r2_recv.at[h, b])
            await_bytes(fw.at[h, b], fw_recv.at[h, b])

            def gathered(other):
                def body(n):
                    at = rows(b, q[h], n, 16)
                    g[at, cols[h]] = (scale * g[at, cols[h]].astype(F32)
                                      + fw[h, b, pl.ds(n, 16)].astype(F32)
                                      + other * r2[h, b, pl.ds(n, 16)].astype(F32)).astype(BF16)
                return body

            strips(up, gathered(after[h]))
            strips(down, lambda n: gathered(before[h])(up + n))
            upper = g.at[rows(b, q[h], 0, up), cols[h]]
            lower = g.at[rows(b, q[h], up, down), cols[h]]

            @pl.when(away == 1)
            def _():
                remote(lower, p2.at[h, pl.ds(up, down)], p_send.at[h], p2_recv.at[h], r_up[h])

            @pl.when(away == 2)
            def _():
                remote(upper, p1.at[h, pl.ds(0, up)], p_send.at[h], p1_recv.at[h], r_up[h])
                remote(lower, p1.at[h, pl.ds(up, down)], p_send.at[h], p1_recv.at[h], r_down[h])

            @pl.when(away == 3)
            def _():
                remote(upper, p2.at[h, pl.ds(0, up)], p_send.at[h], p2_recv.at[h], r_down[h])

    for h in range(2):
        await_bytes(p1.at[h], p1_recv.at[h])

        def upper(n):
            at = rows(turn(r[h], 1), q[h], n, 16)
            g[at, cols[h]] = (g[at, cols[h]].astype(F32) + p1[h, pl.ds(n, 16)].astype(F32)).astype(BF16)

        strips(up, upper)
        remote(g.at[rows(turn(r[h], 1), q[h], 0, up), cols[h]], pf.at[h, pl.ds(0, up)],
               p_send.at[h], pf_recv.at[h], r_up[h])

        def lower(n):
            at = rows(turn(r[h], -1), q[h], up + n, 16)
            g[at, cols[h]] = (g[at, cols[h]].astype(F32) + p1[h, pl.ds(up + n, 16)].astype(F32)).astype(BF16)

        strips(down, lower)
        remote(g.at[rows(turn(r[h], -1), q[h], up, down), cols[h]], pf.at[h, pl.ds(up, down)],
               p_send.at[h], pf_recv.at[h], r_down[h])

    load_n.wait()
    await_bytes(nz.at[0], nz_recv)
    for h in range(2):
        await_bytes(p2.at[h], p2_recv.at[h])
        await_bytes(pf.at[h], pf_recv.at[h])

        def final(n):
            at = pl.ds(n, 16)
            whole = (g[rows(r[h], q[h], n, 16), cols[h]].astype(F32) + p2[h, at].astype(F32)
                     + pf[h, at].astype(F32) + nz[h, at])
            fin[h, at] = (whole * (1.0 / 16.0)).astype(BF16)

        strips(piece, final)
        mine = out_hbm.at[rows(r[h], q[h]), cols[h]]
        remote(fin.at[h], mine, ag1_send.at[h], ag1_recv.at[h, 0], r_up[h])
        remote(fin.at[h], mine, ag1_send.at[h], ag1_recv.at[h, 1], r_down[h])
        remote(fin.at[h], mine, ag2_send.at[h, 0], ag2_recv.at[h, r[h], 0], q_up[h])
        remote(fin.at[h], mine, ag2_send.at[h, 0], ag2_recv.at[h, r[h], 1], q_down[h])
        pltpu.make_async_copy(fin.at[h], mine, own_sem.at[h]).start()

    def place(h, b, p, start=0, size=None):
        return out_hbm.at[rows(b, p, start, size), cols[h]]

    def spread(h, away):
        b = turn(r[h], away)
        at = place(h, b, q[h])
        remote(at, at, ag2_send.at[h, away], ag2_recv.at[h, b, 0], q_up[h])
        remote(at, at, ag2_send.at[h, away], ag2_recv.at[h, b, 1], q_down[h])

    for h in range(2):
        b = turn(r[h], -1)
        await_bytes(place(h, b, q[h]), ag1_recv.at[h, 0])
        at = place(h, b, q[h], 0, up)
        remote(at, at, ag1_send.at[h], ag1_recv.at[h, 2], r_up[h])
        b = turn(r[h], 1)
        await_bytes(place(h, b, q[h]), ag1_recv.at[h, 1])
        at = place(h, b, q[h], up, down)
        remote(at, at, ag1_send.at[h], ag1_recv.at[h, 2], r_down[h])
        spread(h, 3)
        spread(h, 1)

    def relay(h, away):
        b = turn(r[h], away)
        p = turn(q[h], -1)
        await_bytes(place(h, b, p), ag2_recv.at[h, b, 0])
        at = place(h, b, p, 0, up)
        remote(at, at, ag2_send.at[h, away], ag2_recv.at[h, b, 2], q_up[h])
        p = turn(q[h], 1)
        await_bytes(place(h, b, p), ag2_recv.at[h, b, 1])
        at = place(h, b, p, up, down)
        remote(at, at, ag2_send.at[h, away], ag2_recv.at[h, b, 2], q_down[h])

    for h in range(2):
        relay(h, 0)
    for h in range(2):
        b = turn(r[h], 2)
        await_bytes(place(h, b, q[h]), ag1_recv.at[h, 2])
        spread(h, 2)
    for away in (3, 1, 2):
        for h in range(2):
            relay(h, away)
    for away in (0, 3, 1, 2):
        for h in range(2):
            b = turn(r[h], away)
            await_bytes(place(h, b, turn(q[h], 2)), ag2_recv.at[h, b, 2])

    for h in range(2):
        await_bytes(g.at[pl.ds(0, 3 * piece), cols[0]], p_send.at[h])
        await_bytes(g.at[pl.ds(0, 3 * piece), cols[0]], ag1_send.at[h])
        await_bytes(fin.at[h], own_sem.at[h])
        for b in range(RING):
            await_bytes(g.at[pl.ds(0, 2 * piece), cols[0]], raw_send.at[h, b])
            await_bytes(g.at[pl.ds(0, piece), cols[0]], fw_send.at[h, b])
            await_bytes(g.at[pl.ds(0, 3 * piece), cols[0]], ag2_send.at[h, b])
    for side in range(2):
        for m in (4, 5):
            await_bytes(ot_v.at[pl.ds(0, piece)], x_send.at[side, m])
    await_bytes(nrm.at[pl.ds(0, 7)], nrm_send)
    await_bytes(fac.at[pl.ds(1, 4)], fac_send)

    @pl.when(z != y)
    def _():
        await_bytes(nz.at[0], nz_send)


def on_device(hidden, out_grad, lengths, noise):
    _, _, seq_len, units = hidden.shape
    block = out_grad.shape[3]
    width = block * lax.axis_size("tensor")
    layers = lax.axis_size("layer")
    bound = float((seq_len * layers * units * lax.axis_size("tensor") * width / 64.0) ** 0.5)
    positions = lax.broadcasted_iota(jnp.int32, (seq_len, 1), 0)
    valid = positions < lengths[0]
    turned = jnp.where(valid, out_grad[0, 0], jnp.zeros((), BF16)).T
    piece, half = block // RING, units // 2
    dma = pltpu.SemaphoreType.DMA
    result = pl.pallas_call(
        functools.partial(kernel, bound),
        out_shape=jax.ShapeDtypeStruct((width, units), BF16),
        in_specs=[pl.BlockSpec(memory_space=pl.ANY)] * 3,
        out_specs=pl.BlockSpec(memory_space=pl.ANY),
        scratch_shapes=[
            pltpu.VMEM((seq_len, units), BF16),
            pltpu.VMEM((width, seq_len), BF16),
            pltpu.VMEM((width, units), BF16),
            pltpu.VMEM((2, RING, piece, half), BF16),
            pltpu.VMEM((2, RING, piece, half), BF16),
            pltpu.VMEM((2, RING, piece, half), BF16),
            pltpu.VMEM((2, piece, half), BF16),
            pltpu.VMEM((2, piece, half), BF16),
            pltpu.VMEM((2, piece, half), BF16),
            pltpu.VMEM((2, piece, half), F32),
            pltpu.VMEM((2, piece, half), BF16),
            pltpu.VMEM((8, 256), F32),
            pltpu.VMEM((2 * RING, 8, 128), F32),
            pltpu.VMEM((5, 8, 128), F32),
            dma((3,)), dma((2, 6)), dma((2, 6)),
            dma((2, RING)), dma((2, RING)), dma((2, RING)), dma((2, RING)), dma((2, RING)),
            dma((2,)), dma((2,)), dma((2,)), dma((2,)),
            dma, dma, dma, dma, dma, dma,
            dma((2,)), dma((2, 3)), dma((2, RING)), dma((2, RING, 3)), dma((2,)),
        ],
        compiler_params=pltpu.CompilerParams(
            collective_id=0, has_side_effects=True, vmem_limit_bytes=56 * 1024 * 1024
        ),
        cost_estimate=pl.CostEstimate(
            flops=2 * width * units * seq_len, bytes_accessed=30_000_000, transcendentals=0
        ),
    )(turned, hidden[0, 0], noise[0])
    return result[None]


def solution(mesh):
    placed = (
        P("layer", "dp", None, "tensor"),
        P("layer", "dp", None, "tensor"),
        P("dp"),
        P("layer", "dp", "tensor"),
    )
    return jax.shard_map(
        on_device, mesh=mesh, in_specs=placed, out_specs=P("layer", None, "tensor"), check_vma=False
    )
```

```python
import functools

import jax
import jax.numpy as jnp
from jax import lax
from jax.experimental import pallas as pl
from jax.experimental.pallas import tpu as pltpu
from jax.sharding import PartitionSpec as P

MESH = pl.DeviceIdType.MESH
RING = 4
F32 = jnp.float32
BF16 = jnp.bfloat16


def kernel(bound, len_ref, o_hbm, h_hbm, noise_hbm, out,
           h_v, ot_v, g, r1, r2, fw, p1, p2, pf, nz, sq, nrm, fac,
           load_sem, x_send, x_recv, raw_send, r1_recv, r2_recv, fw_send, fw_recv,
           p_send, p1_recv, p2_recv, pf_recv, nrm_send, nrm_recv,
           fac_send, fac_recv, ag1_send, ag1_recv, ag2_send, ag2_recv):
    dp = lax.axis_index("dp")
    x = lax.axis_index("tensor")
    core = lax.axis_index("layer")
    z, y = dp // RING, dp % RING
    block, tokens = o_hbm.shape
    units = h_hbm.shape[1]
    piece = block // RING
    half = units // 2
    up = (piece // 32) * 16 + 16 * (piece // 16 % 2)
    down = piece - up

    def turn(i, by):
        return (i + by + RING) % RING

    z_up, z_down = {"dp": turn(z, 1) * RING + y}, {"dp": turn(z, -1) * RING + y}
    y_up, y_down = {"dp": z * RING + turn(y, 1)}, {"dp": z * RING + turn(y, -1)}
    x_up, x_down = {"tensor": turn(x, 1)}, {"tensor": turn(x, -1)}
    q, r = (z, y), (y, z)
    q_up, q_down = (z_up, y_up), (z_down, y_down)
    r_up, r_down = (y_up, z_up), (y_down, z_down)
    cols = (pl.ds(0, half), pl.ds(half, half))

    def rows(b, p, start=0, size=None):
        return pl.ds(pl.multiple_of(b * block + p * piece + start, 16), piece if size is None else size)

    def chunk(h, u, v, start=0, size=None):
        return rows(u, v, start, size) if h == 0 else rows(v, u, start, size)

    def remote(src, dst, send, recv, device):
        pltpu.make_async_remote_copy(src_ref=src, dst_ref=dst, send_sem=send, recv_sem=recv,
                                     device_id=device, device_id_type=MESH).start()

    def await_bytes(ref, sem):
        pltpu.make_async_copy(ref, ref, sem).wait()

    me = x * 2 + core
    group = []
    for k in range(1, 2 * RING):
        other = (me + k) % (2 * RING)
        group.append({"tensor": other // 2, "layer": other % 2})

    own = pl.multiple_of(x * block, 16)
    load_o = pltpu.make_async_copy(o_hbm, ot_v.at[pl.ds(own, block)], load_sem.at[1])
    load_o.start()
    load_h = pltpu.make_async_copy(h_hbm, h_v, load_sem.at[0])
    load_h.start()
    load_n = pltpu.make_async_copy(noise_hbm, nz, load_sem.at[2])
    load_n.start()

    barrier = pltpu.get_barrier_semaphore()
    for device in group + [z_up, z_down, y_up, y_down]:
        pl.semaphore_signal(barrier, inc=1, device_id=device, device_id_type=MESH)

    pl.semaphore_wait(barrier, 11)

    def passed_on(m):
        return (m == 2) | (m == 4)

    def first(m):
        return jnp.where(m < 2, m, jnp.where(m < 4, jnp.where(m == 2, 0, 2), jnp.where(m == 4, 1, 3)))

    def x_start_up(m):
        at = ot_v.at[rows(jnp.where(passed_on(m), turn(x, -1), x), first(m))]
        remote(at, at, x_send.at[0, m], x_recv.at[0, m], x_up)

    def x_start_down(m):
        at = ot_v.at[rows(jnp.where(passed_on(m), turn(x, 1), x), (first(m) + 2) % RING)]
        remote(at, at, x_send.at[1, m], x_recv.at[1, m], x_down)

    load_o.wait()
    kept = lax.broadcasted_iota(jnp.int32, (16, tokens), 1) < len_ref[0]
    for p in (0, 2, 1, 3):
        @pl.loop(0, piece // 16)
        def _(n):
            at = rows(x, p, n * 16, 16)
            ot_v[at] = jnp.where(kept, ot_v[at], jnp.zeros((), BF16))

        if p < 2:
            x_start_up(jnp.int32(p))
        else:
            x_start_down(jnp.int32(p - 2))

    sq[...] = jnp.zeros_like(sq)
    load_h.wait()

    def product(ba, pa, bb, pb):
        wide = sq.shape[1]

        @pl.loop(0, units // wide)
        def _(n):
            at = pl.ds(pl.multiple_of(n * wide, wide), wide)
            left = jnp.concatenate([ot_v[rows(ba, pa)], ot_v[rows(bb, pb)]], axis=0)
            out = jnp.dot(left, h_v[:, at], preferred_element_type=F32)
            sq[...] += jnp.sum((out * out).reshape(2 * piece // 8, 8, wide), axis=0)
            low = out.astype(BF16)
            g[rows(ba, pa), at] = low[:piece]
            g[rows(bb, pb), at] = low[piece:]

    def send_raw(b, p):
        for h in range(2):
            u, v = (b, p) if h == 0 else (p, b)
            away = turn(u - q[h], 0)
            upper = g.at[rows(b, p, 0, up), cols[h]]
            lower = g.at[rows(b, p, up, down), cols[h]]

            @pl.when(away == 1)
            def _():
                remote(lower, r2.at[h, v, pl.ds(up, down)], raw_send.at[h, v], r2_recv.at[h, v], q_up[h])

            @pl.when(away == 2)
            def _():
                remote(upper, r1.at[h, v, pl.ds(0, up)], raw_send.at[h, v], r1_recv.at[h, v], q_up[h])
                remote(lower, r1.at[h, v, pl.ds(up, down)], raw_send.at[h, v], r1_recv.at[h, v], q_down[h])

            @pl.when(away == 3)
            def _():
                remote(upper, r2.at[h, v, pl.ds(0, up)], raw_send.at[h, v], r2_recv.at[h, v], q_down[h])

    @pl.loop(0, 2)
    def _(i):
        product(x, 2 * i, x, 2 * i + 1)
        send_raw(x, 2 * i)
        send_raw(x, 2 * i + 1)

    @pl.loop(0, 6)
    def _(i):
        ba, pa = jnp.where(passed_on(i), turn(x, 2), turn(x, -1)), first(i)
        bb, pb = jnp.where(passed_on(i), turn(x, 2), turn(x, 1)), (first(i) + 2) % RING
        await_bytes(ot_v.at[rows(ba, pa)], x_recv.at[0, i])
        await_bytes(ot_v.at[rows(bb, pb)], x_recv.at[1, i])

        @pl.when(i < 4)
        def _():
            await_bytes(ot_v.at[pl.ds(0, piece)], x_send.at[0, i])
            await_bytes(ot_v.at[pl.ds(0, piece)], x_send.at[1, i])
            x_start_up(i + 2)
            x_start_down(i + 2)

        product(ba, pa, bb, pb)
        send_raw(ba, pa)
        send_raw(bb, pb)

    nrm[pl.ds(me, 1)] = (sq[:, :128] + sq[:, 128:])[None]
    for device in group:
        remote(nrm.at[me], nrm.at[me], nrm_send, nrm_recv, device)
    await_bytes(nrm.at[pl.ds(0, 7)], nrm_recv)
    total = jnp.sum(jnp.sum(nrm[...], axis=0), keepdims=True)
    factor = jnp.minimum(jnp.float32(1.0), bound / jnp.sqrt(total + 1e-06))
    fac[0] = jnp.broadcast_to(factor, fac.shape[1:])
    for slot, device in ((1, z_up), (2, z_down), (3, y_up), (4, y_down)):
        remote(fac.at[0], fac.at[slot], fac_send, fac_recv, device)
    await_bytes(fac.at[pl.ds(1, 4)], fac_recv)
    scale = fac[0, 0:1, 0:1]
    before = (fac[1, 0:1, 0:1], fac[3, 0:1, 0:1])
    after = (fac[2, 0:1, 0:1], fac[4, 0:1, 0:1])

    def strips(size, body):
        @pl.loop(0, size // 16)
        def _(n):
            body(pl.multiple_of(n * 16, 16))

    def away_of(i):
        return jnp.where(i == 0, 2, jnp.where(i == 1, 1, jnp.where(i == 2, 3, 0)))

    @pl.loop(0, RING)
    def _(i):
        for h in range(2):
            v = turn(r[h], away_of(i))
            await_bytes(r1.at[h, v], r1_recv.at[h, v])

            def upper(n):
                at = chunk(h, turn(q[h], 1), v, n, 16)
                g[at, cols[h]] = (scale * g[at, cols[h]].astype(F32)
                                  + before[h] * r1[h, v, pl.ds(n, 16)].astype(F32)).astype(BF16)

            strips(up, upper)
            remote(g.at[chunk(h, turn(q[h], 1), v, 0, up), cols[h]], fw.at[h, v, pl.ds(0, up)],
                   fw_send.at[h, v], fw_recv.at[h, v], q_up[h])

            def lower(n):
                at = chunk(h, turn(q[h], -1), v, up + n, 16)
                g[at, cols[h]] = (scale * g[at, cols[h]].astype(F32)
                                  + after[h] * r1[h, v, pl.ds(up + n, 16)].astype(F32)).astype(BF16)

            strips(down, lower)
            remote(g.at[chunk(h, turn(q[h], -1), v, up, down), cols[h]], fw.at[h, v, pl.ds(up, down)],
                   fw_send.at[h, v], fw_recv.at[h, v], q_down[h])

    @pl.loop(0, RING)
    def _(i):
        away = away_of(i)
        for h in range(2):
            v = turn(r[h], away)
            await_bytes(r2.at[h, v], r2_recv.at[h, v])
            await_bytes(fw.at[h, v], fw_recv.at[h, v])

            def gathered(other, start):
                def body(n):
                    n = start + n
                    at = chunk(h, q[h], v, n, 16)
                    g[at, cols[h]] = (scale * g[at, cols[h]].astype(F32)
                                      + fw[h, v, pl.ds(n, 16)].astype(F32)
                                      + other * r2[h, v, pl.ds(n, 16)].astype(F32)).astype(BF16)
                return body

            strips(up, gathered(after[h], 0))
            strips(down, gathered(before[h], up))
            upper = g.at[chunk(h, q[h], v, 0, up), cols[h]]
            lower = g.at[chunk(h, q[h], v, up, down), cols[h]]

            @pl.when(away == 1)
            def _():
                remote(lower, p2.at[h, pl.ds(up, down)], p_send.at[h], p2_recv.at[h], r_up[h])

            @pl.when(away == 2)
            def _():
                remote(upper, p1.at[h, pl.ds(0, up)], p_send.at[h], p1_recv.at[h], r_up[h])
                remote(lower, p1.at[h, pl.ds(up, down)], p_send.at[h], p1_recv.at[h], r_down[h])

            @pl.when(away == 3)
            def _():
                remote(upper, p2.at[h, pl.ds(0, up)], p_send.at[h], p2_recv.at[h], r_down[h])

    for h in range(2):
        await_bytes(p1.at[h], p1_recv.at[h])

        def upper(n):
            at = chunk(h, q[h], turn(r[h], 1), n, 16)
            g[at, cols[h]] = (g[at, cols[h]].astype(F32) + p1[h, pl.ds(n, 16)].astype(F32)).astype(BF16)

        strips(up, upper)
        remote(g.at[chunk(h, q[h], turn(r[h], 1), 0, up), cols[h]], pf.at[h, pl.ds(0, up)],
               p_send.at[h], pf_recv.at[h], r_up[h])

        def lower(n):
            at = chunk(h, q[h], turn(r[h], -1), up + n, 16)
            g[at, cols[h]] = (g[at, cols[h]].astype(F32) + p1[h, pl.ds(up + n, 16)].astype(F32)).astype(BF16)

        strips(down, lower)
        remote(g.at[chunk(h, q[h], turn(r[h], -1), up, down), cols[h]], pf.at[h, pl.ds(up, down)],
               p_send.at[h], pf_recv.at[h], r_down[h])

    def place(h, u, v, start=0, size=None):
        return out.at[chunk(h, u, v, start, size), cols[h]]

    def spread(h, away):
        v = turn(r[h], away)
        at = place(h, q[h], v)
        remote(at, at, ag2_send.at[h, away], ag2_recv.at[h, v, 0], q_up[h])
        remote(at, at, ag2_send.at[h, away], ag2_recv.at[h, v, 1], q_down[h])

    load_n.wait()
    for h in range(2):
        await_bytes(p2.at[h], p2_recv.at[h])
        await_bytes(pf.at[h], pf_recv.at[h])

        def final(n):
            at = pl.ds(n, 16)
            whole = (g[chunk(h, q[h], r[h], n, 16), cols[h]].astype(F32) + p2[h, at].astype(F32)
                     + pf[h, at].astype(F32) + nz[at, cols[h]])
            out[chunk(h, q[h], r[h], n, 16), cols[h]] = (whole * (1.0 / 16.0)).astype(BF16)

        strips(piece, final)
        mine = place(h, q[h], r[h])
        remote(mine, mine, ag1_send.at[h], ag1_recv.at[h, 0], r_up[h])
        remote(mine, mine, ag1_send.at[h], ag1_recv.at[h, 1], r_down[h])
        spread(h, 0)

    for h in range(2):
        v = turn(r[h], -1)
        await_bytes(place(h, q[h], v), ag1_recv.at[h, 0])
        at = place(h, q[h], v, 0, up)
        remote(at, at, ag1_send.at[h], ag1_recv.at[h, 2], r_up[h])
        v = turn(r[h], 1)
        await_bytes(place(h, q[h], v), ag1_recv.at[h, 1])
        at = place(h, q[h], v, up, down)
        remote(at, at, ag1_send.at[h], ag1_recv.at[h, 2], r_down[h])
        spread(h, 3)
        spread(h, 1)

    def relay(h, away):
        v = turn(r[h], away)
        u = turn(q[h], -1)
        await_bytes(place(h, u, v), ag2_recv.at[h, v, 0])
        at = place(h, u, v, 0, up)
        remote(at, at, ag2_send.at[h, away], ag2_recv.at[h, v, 2], q_up[h])
        u = turn(q[h], 1)
        await_bytes(place(h, u, v), ag2_recv.at[h, v, 1])
        at = place(h, u, v, up, down)
        remote(at, at, ag2_send.at[h, away], ag2_recv.at[h, v, 2], q_down[h])

    for h in range(2):
        relay(h, 0)
    for h in range(2):
        v = turn(r[h], 2)
        await_bytes(place(h, q[h], v), ag1_recv.at[h, 2])
        spread(h, 2)
    for away in (3, 1, 2):
        for h in range(2):
            relay(h, away)
    for away in (0, 3, 1, 2):
        for h in range(2):
            v = turn(r[h], away)
            await_bytes(place(h, turn(q[h], 2), v), ag2_recv.at[h, v, 2])

    for h in range(2):
        await_bytes(g.at[pl.ds(0, 3 * piece), cols[0]], p_send.at[h])
        await_bytes(g.at[pl.ds(0, 3 * piece), cols[0]], ag1_send.at[h])
        for b in range(RING):
            await_bytes(g.at[pl.ds(0, 2 * piece), cols[0]], raw_send.at[h, b])
            await_bytes(g.at[pl.ds(0, piece), cols[0]], fw_send.at[h, b])
            await_bytes(g.at[pl.ds(0, 3 * piece), cols[0]], ag2_send.at[h, b])
    for side in range(2):
        for m in (4, 5):
            await_bytes(ot_v.at[pl.ds(0, piece)], x_send.at[side, m])
    await_bytes(nrm.at[pl.ds(0, 7)], nrm_send)
    await_bytes(fac.at[pl.ds(1, 4)], fac_send)


def on_device(hidden, out_grad, lengths, noise):
    _, _, seq_len, units = hidden.shape
    block = out_grad.shape[3]
    width = block * lax.axis_size("tensor")
    layers = lax.axis_size("layer")
    bound = float((seq_len * layers * units * lax.axis_size("tensor") * width / 64.0) ** 0.5)
    piece, half = block // RING, units // 2
    dma = pltpu.SemaphoreType.DMA
    result = pl.pallas_call(
        functools.partial(kernel, bound),
        out_shape=pltpu.VMEM((width, units), BF16),
        in_specs=[pl.BlockSpec(memory_space=pltpu.SMEM)] + [pl.BlockSpec(memory_space=pltpu.HBM)] * 3,
        out_specs=pl.BlockSpec(memory_space=pltpu.VMEM),
        scratch_shapes=[
            pltpu.VMEM((seq_len, units), BF16),
            pltpu.VMEM((width, seq_len), BF16),
            pltpu.VMEM((width, units), BF16),
            pltpu.VMEM((2, RING, piece, half), BF16),
            pltpu.VMEM((2, RING, piece, half), BF16),
            pltpu.VMEM((2, RING, piece, half), BF16),
            pltpu.VMEM((2, piece, half), BF16),
            pltpu.VMEM((2, piece, half), BF16),
            pltpu.VMEM((2, piece, half), BF16),
            pltpu.VMEM((piece, units), F32),
            pltpu.VMEM((8, 256), F32),
            pltpu.VMEM((2 * RING, 8, 128), F32),
            pltpu.VMEM((5, 8, 128), F32),
            dma((3,)), dma((2, 6)), dma((2, 6)),
            dma((2, RING)), dma((2, RING)), dma((2, RING)), dma((2, RING)), dma((2, RING)),
            dma((2,)), dma((2,)), dma((2,)), dma((2,)),
            dma, dma, dma, dma,
            dma((2,)), dma((2, 3)), dma((2, RING)), dma((2, RING, 3)),
        ],
        compiler_params=pltpu.CompilerParams(
            collective_id=0, has_side_effects=True, vmem_limit_bytes=40 * 1024 * 1024
        ),
        cost_estimate=pl.CostEstimate(
            flops=2 * width * units * seq_len, bytes_accessed=30_000_000, transcendentals=0
        ),
    )(lengths, *(pltpu.with_memory_space_constraint(a, pltpu.HBM) for a in (out_grad[0, 0].T, hidden[0, 0], noise[0])))
    return result[None]


def solution(mesh):
    placed = (
        P("layer", "dp", None, "tensor"),
        P("layer", "dp", None, "tensor"),
        P("dp"),
        P("layer", "dp", "tensor"),
    )
    return jax.shard_map(
        on_device, mesh=mesh, in_specs=placed, out_specs=P("layer", None, "tensor"), check_vma=False
    )
```

```python
import functools

import jax
import jax.numpy as jnp
from jax import lax
from jax.experimental import pallas as pl
from jax.experimental.pallas import tpu as pltpu
from jax.sharding import PartitionSpec as P

MESH = pl.DeviceIdType.MESH
RING = 4
F32 = jnp.float32
BF16 = jnp.bfloat16


def kernel(bound, len_ref, o_hbm, h_hbm, noise_hbm, out,
           h_v, ot_v, g, r1, from_down, from_up, fw, p1, p2, pf, nz, sq, nrm, fac,
           load_sem, x_send, x_recv, raw_send, r1_recv, r2_recv, fw_send, fw_recv,
           p_send, p1_recv, p2_recv, pf_recv, nrm_send, nrm_recv,
           fac_send, fac_recv, ag1_send, ag1_recv, ag2_send, ag2_recv):
    dp = lax.axis_index("dp")
    x = lax.axis_index("tensor")
    core = lax.axis_index("layer")
    z, y = dp // RING, dp % RING
    block, tokens = o_hbm.shape
    units = h_hbm.shape[1]
    piece = block // RING
    half = units // 2
    cuts = (piece - piece // 32 * 16, piece // 32 * 16)

    def turn(i, by):
        return (i + by + RING) % RING

    z_up, z_down = {"dp": turn(z, 1) * RING + y}, {"dp": turn(z, -1) * RING + y}
    y_up, y_down = {"dp": z * RING + turn(y, 1)}, {"dp": z * RING + turn(y, -1)}
    x_up, x_down = {"tensor": turn(x, 1)}, {"tensor": turn(x, -1)}
    z_far, y_far = {"dp": turn(z, 2) * RING + y}, {"dp": z * RING + turn(y, 2)}
    q, r = (z, y), (y, z)
    q_up, q_down, q_far = (z_up, y_up), (z_down, y_down), (z_far, y_far)
    r_up, r_down = (y_up, z_up), (y_down, z_down)
    cols = (pl.ds(0, half), pl.ds(half, half))

    def rows(b, p, start=0, size=None):
        return pl.ds(pl.multiple_of(b * block + p * piece + start, 16), piece if size is None else size)

    def chunk(h, u, v, start=0, size=None):
        return rows(u, v, start, size) if h == 0 else rows(v, u, start, size)

    def remote(src, dst, send, recv, device):
        pltpu.make_async_remote_copy(src_ref=src, dst_ref=dst, send_sem=send, recv_sem=recv,
                                     device_id=device, device_id_type=MESH).start()

    def await_bytes(ref, sem):
        pltpu.make_async_copy(ref, ref, sem).wait()

    me = x * 2 + core
    group = []
    for k in range(1, 2 * RING):
        other = (me + k) % (2 * RING)
        group.append({"tensor": other // 2, "layer": other % 2})

    own = pl.multiple_of(x * block, 16)
    load_o = pltpu.make_async_copy(o_hbm, ot_v.at[pl.ds(own, block)], load_sem.at[1])
    load_o.start()
    load_h = pltpu.make_async_copy(h_hbm, h_v, load_sem.at[0])
    load_h.start()
    load_n = pltpu.make_async_copy(noise_hbm, nz, load_sem.at[2])
    load_n.start()

    barrier = pltpu.get_barrier_semaphore()
    for device in group + [z_up, z_down, z_far, y_up, y_down, y_far]:
        pl.semaphore_signal(barrier, inc=1, device_id=device, device_id_type=MESH)

    pl.semaphore_wait(barrier, 13)

    def passed_on(m):
        return (m == 2) | (m == 5)

    def first(m):
        return jnp.where((m == 0) | (m == 2), 0, jnp.where(m == 1, 2, jnp.where(m == 4, 3, 1)))

    def x_start_up(m):
        at = ot_v.at[rows(jnp.where(passed_on(m), turn(x, -1), x), first(m))]
        remote(at, at, x_send.at[0, m], x_recv.at[0, m], x_up)

    def x_start_down(m):
        at = ot_v.at[rows(jnp.where(passed_on(m), turn(x, 1), x), (first(m) + 2) % RING)]
        remote(at, at, x_send.at[1, m], x_recv.at[1, m], x_down)

    load_o.wait()
    kept = lax.broadcasted_iota(jnp.int32, (16, tokens), 1) < len_ref[0]
    for p in (0, 2, 1, 3):
        @pl.loop(0, piece // 16)
        def _(n):
            at = rows(x, p, n * 16, 16)
            ot_v[at] = jnp.where(kept, ot_v[at], jnp.zeros((), BF16))

        if p == 2:
            for m in range(2):
                x_start_up(jnp.int32(m))
                x_start_down(jnp.int32(m))

    sq[...] = jnp.zeros_like(sq)
    load_h.wait()

    def kind(h, b, p):
        if h == 0:
            return p // 2, p % 2 == 0
        ahead = turn(b - x, 0)
        return ahead // 2, (ahead == 0) | (ahead == 3)

    def send_raw(h, b, p):
        u, v = (b, p) if h == 0 else (p, b)
        away = turn(u - q[h], 0)
        cut, direct = kind(h, b, p)
        whole = g.at[rows(b, p), cols[h]]

        @pl.when(direct & (away == 1))
        def _():
            remote(whole, from_down.at[h, v], raw_send.at[h, v], r2_recv.at[h, v], q_up[h])

        @pl.when(direct & (away == 3))
        def _():
            remote(whole, from_up.at[h, v], raw_send.at[h, v], r2_recv.at[h, v], q_down[h])

        for k, up in enumerate(cuts):
            upper, lower = g.at[rows(b, p, 0, up), cols[h]], g.at[rows(b, p, up, piece - up), cols[h]]
            above, below = pl.ds(0, up), pl.ds(up, piece - up)

            @pl.when((cut == k) & ~direct & (away == 1))
            def _():
                remote(lower, from_down.at[h, v, below], raw_send.at[h, v], r2_recv.at[h, v], q_up[h])

            @pl.when((cut == k) & ~direct & (away == 3))
            def _():
                remote(upper, from_up.at[h, v, above], raw_send.at[h, v], r2_recv.at[h, v], q_down[h])

            @pl.when((cut == k) & (away == 2))
            def _():
                remote(upper, r1.at[h, v, above], raw_send.at[h, v], r1_recv.at[h, v], q_up[h])
                remote(lower, r1.at[h, v, below], raw_send.at[h, v], r1_recv.at[h, v], q_down[h])

    def product(ba, pa, bb, pb):
        for h in range(2):
            left = jnp.concatenate([ot_v[rows(ba, pa)], ot_v[rows(bb, pb)]], axis=0)
            result = jnp.dot(left, h_v[:, cols[h]], preferred_element_type=F32)
            sq[...] += jnp.sum((result * result).reshape(2 * piece // 8, 8, half), axis=0)
            low = result.astype(BF16)
            g[rows(ba, pa), cols[h]] = low[:piece]
            g[rows(bb, pb), cols[h]] = low[piece:]
            send_raw(h, ba, pa)
            send_raw(h, bb, pb)

    def second(h, rel):
        return rel if h == 0 else turn(x, rel)

    def relay_raw(h, rel):
        v = second(h, rel)
        up = cuts[rel // 2]
        await_bytes(r1.at[h, v], r1_recv.at[h, v])
        remote(r1.at[h, v, pl.ds(0, up)], fw.at[h, v, pl.ds(0, up)], fw_send.at[h, v], fw_recv.at[h, v], q_up[h])
        remote(r1.at[h, v, pl.ds(up, piece - up)], fw.at[h, v, pl.ds(up, piece - up)],
               fw_send.at[h, v], fw_recv.at[h, v], q_down[h])

    @pl.loop(0, 2)
    def _(i):
        product(x, 2 * i, x, 2 * i + 1)

    @pl.loop(0, 6)
    def _(i):
        ba, pa = jnp.where(passed_on(i), turn(x, 2), turn(x, -1)), first(i)
        bb, pb = jnp.where(passed_on(i), turn(x, 2), turn(x, 1)), (first(i) + 2) % RING
        await_bytes(ot_v.at[rows(ba, pa)], x_recv.at[0, i])
        await_bytes(ot_v.at[rows(bb, pb)], x_recv.at[1, i])

        @pl.when(i < 4)
        def _():
            await_bytes(ot_v.at[pl.ds(0, piece)], x_send.at[0, i])
            await_bytes(ot_v.at[pl.ds(0, piece)], x_send.at[1, i])
            x_start_up(i + 2)
            x_start_down(i + 2)

        product(ba, pa, bb, pb)

        @pl.when(i == 1)
        def _():
            relay_raw(1, 0)

        @pl.when(i == 3)
        def _():
            relay_raw(0, 0)
            relay_raw(0, 2)

    relay_raw(1, 3)

    nrm[pl.ds(me, 1)] = sum(sq[:, k:k + 128] for k in range(0, half, 128))[None]
    for device in group:
        remote(nrm.at[me], nrm.at[me], nrm_send, nrm_recv, device)
    await_bytes(nrm.at[pl.ds(0, 7)], nrm_recv)
    total = jnp.sum(jnp.sum(nrm[...], axis=0), keepdims=True)
    factor = jnp.minimum(jnp.float32(1.0), bound / jnp.sqrt(total + 1e-06))
    fac[0] = jnp.broadcast_to(factor, fac.shape[1:])
    for slot, device in ((1, z_up), (2, z_down), (3, z_far), (4, y_up), (5, y_down), (6, y_far)):
        remote(fac.at[0], fac.at[slot], fac_send, fac_recv, device)
    await_bytes(fac.at[pl.ds(1, 6)], fac_recv)
    scale = fac[0, 0:1, 0:1]
    before, after, far = ([fac[k + 3 * h, 0:1, 0:1] for h in range(2)] for k in (1, 2, 3))

    def strips(size, body):
        @pl.loop(0, size // 16)
        def _(n):
            body(pl.multiple_of(n * 16, 16))

    def pass_on(h, rel):
        v = second(h, rel)
        up = cuts[rel // 2]
        await_bytes(r1.at[h, v], r1_recv.at[h, v])

        def upper(n):
            at = chunk(h, turn(q[h], 1), v, n, 16)
            g[at, cols[h]] = (scale * g[at, cols[h]].astype(F32)
                              + before[h] * r1[h, v, pl.ds(n, 16)].astype(F32)).astype(BF16)

        strips(up, upper)
        remote(g.at[chunk(h, turn(q[h], 1), v, 0, up), cols[h]], fw.at[h, v, pl.ds(0, up)],
               fw_send.at[h, v], fw_recv.at[h, v], q_up[h])

        def lower(n):
            at = chunk(h, turn(q[h], -1), v, up + n, 16)
            g[at, cols[h]] = (scale * g[at, cols[h]].astype(F32)
                              + after[h] * r1[h, v, pl.ds(up + n, 16)].astype(F32)).astype(BF16)

        strips(piece - up, lower)
        remote(g.at[chunk(h, turn(q[h], -1), v, up, piece - up), cols[h]], fw.at[h, v, pl.ds(up, piece - up)],
               fw_send.at[h, v], fw_recv.at[h, v], q_down[h])

    upper_p, lower_p = pl.ds(0, cuts[0]), pl.ds(cuts[0], piece - cuts[0])

    def send_second(h, v):
        away = turn(v - r[h], 0)
        upper = g.at[chunk(h, q[h], v, 0, cuts[0]), cols[h]]
        lower = g.at[chunk(h, q[h], v, cuts[0], piece - cuts[0]), cols[h]]

        @pl.when(away == 1)
        def _():
            remote(lower, p2.at[h, lower_p], p_send.at[h], p2_recv.at[h], r_up[h])

        @pl.when(away == 2)
        def _():
            remote(upper, p1.at[h, upper_p], p_send.at[h], p1_recv.at[h], r_up[h])
            remote(lower, p1.at[h, lower_p], p_send.at[h], p1_recv.at[h], r_down[h])

        @pl.when(away == 3)
        def _():
            remote(upper, p2.at[h, upper_p], p_send.at[h], p2_recv.at[h], r_down[h])

    def gather_direct(h, rel):
        v = second(h, rel)
        await_bytes(g.at[pl.ds(0, 2 * piece), cols[h]], r2_recv.at[h, v])
        await_bytes(fw.at[h, v], fw_recv.at[h, v])

        def body(n):
            at, part = chunk(h, q[h], v, n, 16), pl.ds(n, 16)
            g[at, cols[h]] = (scale * g[at, cols[h]].astype(F32) + far[h] * fw[h, v, part].astype(F32)
                              + before[h] * from_down[h, v, part].astype(F32)
                              + after[h] * from_up[h, v, part].astype(F32)).astype(BF16)

        strips(piece, body)
        send_second(h, v)

    def gather_passed(h, rel):
        v = second(h, rel)
        up = cuts[rel // 2]
        await_bytes(g.at[pl.ds(0, piece), cols[h]], r2_recv.at[h, v])
        await_bytes(fw.at[h, v], fw_recv.at[h, v])

        def gathered(other, ref, start):
            def body(n):
                n = start + n
                at, part = chunk(h, q[h], v, n, 16), pl.ds(n, 16)
                g[at, cols[h]] = (scale * g[at, cols[h]].astype(F32) + fw[h, v, part].astype(F32)
                                  + other * ref[h, v, part].astype(F32)).astype(BF16)
            return body

        strips(up, gathered(after[h], from_up, 0))
        strips(piece - up, gathered(before[h], from_down, up))
        send_second(h, v)

    for h, rel in ((1, 1), (0, 1), (0, 3), (1, 2)):
        pass_on(h, rel)
    for h, rel in ((0, 0), (1, 0), (0, 2), (1, 3)):
        gather_direct(h, rel)
    for h, rel in ((1, 1), (0, 1), (0, 3), (1, 2)):
        gather_passed(h, rel)

    up, down = cuts[0], piece - cuts[0]
    for h in range(2):
        await_bytes(p1.at[h], p1_recv.at[h])

        def upper(n):
            at = chunk(h, q[h], turn(r[h], 1), n, 16)
            g[at, cols[h]] = (g[at, cols[h]].astype(F32) + p1[h, pl.ds(n, 16)].astype(F32)).astype(BF16)

        strips(up, upper)
        remote(g.at[chunk(h, q[h], turn(r[h], 1), 0, up), cols[h]], pf.at[h, pl.ds(0, up)],
               p_send.at[h], pf_recv.at[h], r_up[h])

        def lower(n):
            at = chunk(h, q[h], turn(r[h], -1), up + n, 16)
            g[at, cols[h]] = (g[at, cols[h]].astype(F32) + p1[h, pl.ds(up + n, 16)].astype(F32)).astype(BF16)

        strips(down, lower)
        remote(g.at[chunk(h, q[h], turn(r[h], -1), up, down), cols[h]], pf.at[h, pl.ds(up, down)],
               p_send.at[h], pf_recv.at[h], r_down[h])

    def place(h, u, v, start=0, size=None):
        return out.at[chunk(h, u, v, start, size), cols[h]]

    def spread(h, away):
        v = turn(r[h], away)
        at = place(h, q[h], v)
        remote(at, at, ag2_send.at[h, away], ag2_recv.at[h, v, 0], q_up[h])
        remote(at, at, ag2_send.at[h, away], ag2_recv.at[h, v, 1], q_down[h])

    load_n.wait()
    for h in range(2):
        await_bytes(p2.at[h], p2_recv.at[h])
        await_bytes(pf.at[h], pf_recv.at[h])

        def final(n):
            at = pl.ds(n, 16)
            whole = (g[chunk(h, q[h], r[h], n, 16), cols[h]].astype(F32) + p2[h, at].astype(F32)
                     + pf[h, at].astype(F32) + nz[at, cols[h]])
            out[chunk(h, q[h], r[h], n, 16), cols[h]] = (whole * (1.0 / 16.0)).astype(BF16)

        strips(piece, final)
        mine = place(h, q[h], r[h])
        remote(mine, mine, ag1_send.at[h], ag1_recv.at[h, 0], r_up[h])
        remote(mine, mine, ag1_send.at[h], ag1_recv.at[h, 1], r_down[h])
        spread(h, 0)

    for h in range(2):
        v = turn(r[h], -1)
        await_bytes(place(h, q[h], v), ag1_recv.at[h, 0])
        at = place(h, q[h], v, 0, up)
        remote(at, at, ag1_send.at[h], ag1_recv.at[h, 2], r_up[h])
        v = turn(r[h], 1)
        await_bytes(place(h, q[h], v), ag1_recv.at[h, 1])
        at = place(h, q[h], v, up, down)
        remote(at, at, ag1_send.at[h], ag1_recv.at[h, 2], r_down[h])
        spread(h, 3)
        spread(h, 1)

    def relay(h, away):
        v = turn(r[h], away)
        up = cuts[away % 2]
        u = turn(q[h], -1)
        await_bytes(place(h, u, v), ag2_recv.at[h, v, 0])
        at = place(h, u, v, 0, up)
        remote(at, at, ag2_send.at[h, away], ag2_recv.at[h, v, 2], q_up[h])
        u = turn(q[h], 1)
        await_bytes(place(h, u, v), ag2_recv.at[h, v, 1])
        at = place(h, u, v, up, piece - up)
        remote(at, at, ag2_send.at[h, away], ag2_recv.at[h, v, 2], q_down[h])

    for h in range(2):
        relay(h, 0)
    for h in range(2):
        v = turn(r[h], 2)
        await_bytes(place(h, q[h], v), ag1_recv.at[h, 2])
        spread(h, 2)
    for away in (3, 1, 2):
        for h in range(2):
            relay(h, away)
    for away in (0, 3, 1, 2):
        for h in range(2):
            v = turn(r[h], away)
            await_bytes(place(h, turn(q[h], 2), v), ag2_recv.at[h, v, 2])

    for h in range(2):
        await_bytes(g.at[pl.ds(0, 3 * piece), cols[0]], p_send.at[h])
        await_bytes(g.at[pl.ds(0, 3 * piece), cols[0]], ag1_send.at[h])
        for rel in range(RING):
            rows_out = (3 if (rel % 2 == 0 if h == 0 else rel in (0, 3)) else 2) * piece
            await_bytes(g.at[pl.ds(0, rows_out), cols[0]], raw_send.at[h, second(h, rel)])
        for b in range(RING):
            await_bytes(g.at[pl.ds(0, piece), cols[0]], fw_send.at[h, b])
            await_bytes(g.at[pl.ds(0, 3 * piece), cols[0]], ag2_send.at[h, b])
    for side in range(2):
        for m in (4, 5):
            await_bytes(ot_v.at[pl.ds(0, piece)], x_send.at[side, m])
    await_bytes(nrm.at[pl.ds(0, 7)], nrm_send)
    await_bytes(fac.at[pl.ds(1, 6)], fac_send)


def on_device(hidden, out_grad, lengths, noise):
    _, _, seq_len, units = hidden.shape
    block = out_grad.shape[3]
    width = block * lax.axis_size("tensor")
    layers = lax.axis_size("layer")
    bound = float((seq_len * layers * units * lax.axis_size("tensor") * width / 64.0) ** 0.5)
    piece, half = block // RING, units // 2
    dma = pltpu.SemaphoreType.DMA
    result = pl.pallas_call(
        functools.partial(kernel, bound),
        out_shape=pltpu.VMEM((width, units), BF16),
        in_specs=[pl.BlockSpec(memory_space=pltpu.SMEM)] + [pl.BlockSpec(memory_space=pltpu.HBM)] * 3,
        out_specs=pl.BlockSpec(memory_space=pltpu.VMEM),
        scratch_shapes=[
            pltpu.VMEM((seq_len, units), BF16),
            pltpu.VMEM((width, seq_len), BF16),
            pltpu.VMEM((width, units), BF16),
            pltpu.VMEM((2, RING, piece, half), BF16),
            pltpu.VMEM((2, RING, piece, half), BF16),
            pltpu.VMEM((2, RING, piece, half), BF16),
            pltpu.VMEM((2, RING, piece, half), BF16),
            pltpu.VMEM((2, piece, half), BF16),
            pltpu.VMEM((2, piece, half), BF16),
            pltpu.VMEM((2, piece, half), BF16),
            pltpu.VMEM((piece, units), F32),
            pltpu.VMEM((8, half), F32),
            pltpu.VMEM((2 * RING, 8, 128), F32),
            pltpu.VMEM((7, 8, 128), F32),
            dma((3,)), dma((2, 6)), dma((2, 6)),
            dma((2, RING)), dma((2, RING)), dma((2, RING)), dma((2, RING)), dma((2, RING)),
            dma((2,)), dma((2,)), dma((2,)), dma((2,)),
            dma, dma, dma, dma,
            dma((2,)), dma((2, 3)), dma((2, RING)), dma((2, RING, 3)),
        ],
        compiler_params=pltpu.CompilerParams(
            collective_id=0, has_side_effects=True, vmem_limit_bytes=44 * 1024 * 1024
        ),
        cost_estimate=pl.CostEstimate(
            flops=2 * width * units * seq_len, bytes_accessed=30_000_000, transcendentals=0
        ),
    )(lengths, *(pltpu.with_memory_space_constraint(a, pltpu.HBM) for a in (out_grad[0, 0].T, hidden[0, 0], noise[0])))
    return result[None]


def solution(mesh):
    placed = (
        P("layer", "dp", None, "tensor"),
        P("layer", "dp", None, "tensor"),
        P("dp"),
        P("layer", "dp", "tensor"),
    )
    return jax.shard_map(
        on_device, mesh=mesh, in_specs=placed, out_specs=P("layer", None, "tensor"), check_vma=False
    )
```

```python
import functools

import jax
import jax.numpy as jnp
from jax import lax
from jax.experimental import pallas as pl
from jax.experimental.pallas import tpu as pltpu
from jax.sharding import PartitionSpec as P

MESH = pl.DeviceIdType.MESH
RING = 4
F32 = jnp.float32
DIRECT = ((0,), (0,))
BF16 = jnp.bfloat16


def kernel(bound, len_ref, o_hbm, h_hbm, noise_hbm, out,
           h_v, ot_v, g, r1, from_down, from_up, fw, p1, p2, pf, nz, nz_low, nz_mid, sq, nrm, fac,
           load_sem, x_send, x_recv, raw_send, r1_recv, r2_recv, fw_send, fw_recv,
           p_send, p1_recv, p2_recv, pf_recv, nz_send, nz_recv, mid_send, mid_recv, nrm_send, nrm_recv,
           fac_send, fac_recv, ag1_send, ag1_recv, ag2_send, ag2_recv):
    dp = lax.axis_index("dp")
    x = lax.axis_index("tensor")
    core = lax.axis_index("layer")
    z, y = dp // RING, dp % RING
    block, tokens = o_hbm.shape
    units = h_hbm.shape[1]
    piece = block // RING
    half = units // 2
    cuts = (piece - piece // 32 * 16, piece // 32 * 16)

    def turn(i, by):
        return (i + by + RING) % RING

    z_up, z_down = {"dp": turn(z, 1) * RING + y}, {"dp": turn(z, -1) * RING + y}
    y_up, y_down = {"dp": z * RING + turn(y, 1)}, {"dp": z * RING + turn(y, -1)}
    x_up, x_down = {"tensor": turn(x, 1)}, {"tensor": turn(x, -1)}
    z_far, y_far = {"dp": turn(z, 2) * RING + y}, {"dp": z * RING + turn(y, 2)}
    q, r = (z, y), (y, z)
    q_up, q_down, q_far = (z_up, y_up), (z_down, y_down), (z_far, y_far)
    r_up, r_down = (y_up, z_up), (y_down, z_down)
    cols = (pl.ds(0, half), pl.ds(half, half))

    def rows(b, p, start=0, size=None):
        return pl.ds(pl.multiple_of(b * block + p * piece + start, 16), piece if size is None else size)

    def chunk(u, v, start=0, size=None):
        return rows(v, u, start, size)

    def remote(src, dst, send, recv, device):
        pltpu.make_async_remote_copy(src_ref=src, dst_ref=dst, send_sem=send, recv_sem=recv,
                                     device_id=device, device_id_type=MESH).start()

    def await_bytes(ref, sem):
        pltpu.make_async_copy(ref, ref, sem).wait()

    me = x * 2 + core
    group = []
    for k in range(1, 2 * RING):
        other = (me + k) % (2 * RING)
        group.append({"tensor": other // 2, "layer": other % 2})

    own = pl.multiple_of(x * block, 16)
    load_o = pltpu.make_async_copy(o_hbm, ot_v.at[pl.ds(own, block)], load_sem.at[1])
    load_o.start()
    load_h = pltpu.make_async_copy(h_hbm, h_v, load_sem.at[0])
    load_h.start()
    load_n = pltpu.make_async_copy(noise_hbm, nz, load_sem.at[2])
    load_n.start()

    barrier = pltpu.get_barrier_semaphore()
    for device in group + [z_up, z_down, z_far, y_up, y_down, y_far]:
        pl.semaphore_signal(barrier, inc=1, device_id=device, device_id_type=MESH)

    def passed_on(m):
        return m >= RING

    def first(m):
        return jnp.where((m == 0) | (m == 4), 0, jnp.where(m == 1, 2, jnp.where(m == 3, 3, 1)))

    def x_start_up(m):
        at = ot_v.at[rows(jnp.where(passed_on(m), turn(x, -1), x), first(m))]
        remote(at, at, x_send.at[0, m], x_recv.at[0, m], x_up)

    def x_start_down(m):
        at = ot_v.at[rows(jnp.where(passed_on(m), turn(x, 1), x), (first(m) + 2) % RING)]
        remote(at, at, x_send.at[1, m], x_recv.at[1, m], x_down)

    load_o.wait()
    kept = lax.broadcasted_iota(jnp.int32, (16, tokens), 1) < len_ref[0]

    @pl.loop(0, block // 16)
    def _(n):
        at = rows(x, 0, n * 16, 16)
        ot_v[at] = jnp.where(kept, ot_v[at], jnp.zeros((), BF16))

    sq[...] = jnp.zeros_like(sq)
    pl.semaphore_wait(barrier, 13)
    for m in range(2):
        x_start_up(jnp.int32(m))
        x_start_down(jnp.int32(m))

    load_n.wait()

    @pl.loop(0, piece // 16)
    def _(n):
        at = pl.ds(pl.multiple_of(n * 16, 16), 16)
        low = nz[at, cols[0]].astype(BF16)
        nz_low[0, at] = low

        @pl.when(z == y)
        def _():
            nz_low[1, at] = low

    above, below = pl.ds(0, cuts[0]), pl.ds(cuts[0], piece - cuts[0])

    @pl.when(z != y)
    def _():
        remote(nz_low.at[0, above], nz_mid.at[z, above], nz_send, mid_recv, {"dp": y * RING + y})
        remote(nz_low.at[0, below], nz_mid.at[y, below], nz_send, mid_recv, {"dp": z * RING + z})

    load_h.wait()

    def kind(h, b):
        ahead = turn(b - x, 0)
        direct = ahead == DIRECT[h][0]
        for rel in DIRECT[h][1:]:
            direct = direct | (ahead == rel)
        return ahead // 2, direct

    def send_raw(h, v, u):
        b, p = v, u
        away = turn(u - q[h], 0)
        cut, direct = kind(h, b)
        whole = g.at[rows(b, p), cols[h]]

        @pl.when(direct & (away == 1))
        def _():
            remote(whole, from_down.at[h, v], raw_send.at[h, v], r2_recv.at[h, v], q_up[h])

        @pl.when(direct & (away == 3))
        def _():
            remote(whole, from_up.at[h, v], raw_send.at[h, v], r2_recv.at[h, v], q_down[h])

        for k, up in enumerate(cuts):
            upper, lower = g.at[rows(b, p, 0, up), cols[h]], g.at[rows(b, p, up, piece - up), cols[h]]
            above, below = pl.ds(0, up), pl.ds(up, piece - up)

            @pl.when((cut == k) & ~direct & (away == 1))
            def _():
                remote(lower, from_down.at[h, v, below], raw_send.at[h, v], r2_recv.at[h, v], q_up[h])

            @pl.when((cut == k) & ~direct & (away == 3))
            def _():
                remote(upper, from_up.at[h, v, above], raw_send.at[h, v], r2_recv.at[h, v], q_down[h])

            @pl.when((cut == k) & (away == 2))
            def _():
                remote(upper, r1.at[h, v, above], raw_send.at[h, v], r1_recv.at[h, v], q_up[h])
                remote(lower, r1.at[h, v, below], raw_send.at[h, v], r1_recv.at[h, v], q_down[h])

    def product(ba, pa, bb, pb):
        for h in range(2):
            left = jnp.concatenate([ot_v[rows(ba, pa)], ot_v[rows(bb, pb)]], axis=0)
            result = jnp.dot(left, h_v[:, cols[h]], preferred_element_type=F32)
            sq[...] += jnp.sum((result * result).reshape(2 * piece // 8, 8, half), axis=0)
            low = result.astype(BF16)
            g[rows(ba, pa), cols[h]] = low[:piece]
            g[rows(bb, pb), cols[h]] = low[piece:]
            send_raw(h, ba, pa)
            send_raw(h, bb, pb)

    def second(h, rel):
        return turn(x, rel)

    def relay_raw(h, rel):
        v = second(h, rel)
        up = cuts[rel // 2]
        await_bytes(r1.at[h, v], r1_recv.at[h, v])
        remote(r1.at[h, v, pl.ds(0, up)], fw.at[h, v, pl.ds(0, up)], fw_send.at[h, v], fw_recv.at[h, v], q_up[h])
        remote(r1.at[h, v, pl.ds(up, piece - up)], fw.at[h, v, pl.ds(up, piece - up)],
               fw_send.at[h, v], fw_recv.at[h, v], q_down[h])

    @pl.loop(0, 2)
    def _(i):
        product(x, 2 * i, x, 2 * i + 1)

    @pl.when(z == y)
    def _():
        await_bytes(nz_mid.at[pl.ds(0, 3)], mid_recv)
        for k in range(1, RING):
            other = turn(z, k)
            remote(nz_mid.at[other, above], nz_low.at[1, above], mid_send, nz_recv, {"dp": z * RING + other})
            remote(nz_mid.at[other, below], nz_low.at[1, below], mid_send, nz_recv, {"dp": other * RING + z})

    @pl.loop(0, 6)
    def _(i):
        ba, pa = jnp.where(passed_on(i), turn(x, 2), turn(x, -1)), first(i)
        bb, pb = jnp.where(passed_on(i), turn(x, 2), turn(x, 1)), (first(i) + 2) % RING
        await_bytes(ot_v.at[rows(ba, pa)], x_recv.at[0, i])
        await_bytes(ot_v.at[rows(bb, pb)], x_recv.at[1, i])

        @pl.when(i < 4)
        def _():
            await_bytes(ot_v.at[pl.ds(0, piece)], x_send.at[0, i])
            await_bytes(ot_v.at[pl.ds(0, piece)], x_send.at[1, i])
            x_start_up(i + 2)
            x_start_down(i + 2)

        product(ba, pa, bb, pb)

        @pl.when(i == 1)
        def _():
            for h in range(2):
                relay_raw(h, 0)

        @pl.when(i == 4)
        def _():
            for h in range(2):
                for rel in DIRECT[h][1:]:
                    relay_raw(h, rel)

    nrm[pl.ds(me, 1)] = sum(sq[:, k:k + 128] for k in range(0, half, 128))[None]
    for device in group:
        remote(nrm.at[me], nrm.at[me], nrm_send, nrm_recv, device)
    await_bytes(nrm.at[pl.ds(0, 7)], nrm_recv)
    total = jnp.sum(jnp.sum(nrm[...], axis=0), keepdims=True)
    factor = jnp.minimum(jnp.float32(1.0), bound / jnp.sqrt(total + 1e-06))
    fac[0] = jnp.broadcast_to(factor, fac.shape[1:])
    for slot, device in ((1, z_up), (2, z_down), (3, z_far), (4, y_up), (5, y_down), (6, y_far)):
        remote(fac.at[0], fac.at[slot], fac_send, fac_recv, device)
    await_bytes(fac.at[pl.ds(1, 6)], fac_recv)
    scale = fac[0, 0:1, 0:1]
    before, after, far = ([fac[k + 3 * h, 0:1, 0:1] for h in range(2)] for k in (1, 2, 3))

    def strips(size, body):
        @pl.loop(0, size // 16)
        def _(n):
            body(pl.multiple_of(n * 16, 16))

    def away_of(i):
        return jnp.where(i == 0, 2, jnp.where(i == 1, 1, jnp.where(i == 2, 3, 0)))

    def pass_on(h, v, up):
        await_bytes(r1.at[h, v], r1_recv.at[h, v])

        def upper(n):
            at = chunk(turn(q[h], 1), v, n, 16)
            g[at, cols[h]] = (scale * g[at, cols[h]].astype(F32)
                              + before[h] * r1[h, v, pl.ds(n, 16)].astype(F32)).astype(BF16)

        strips(up, upper)
        remote(g.at[chunk(turn(q[h], 1), v, 0, up), cols[h]], fw.at[h, v, pl.ds(0, up)],
               fw_send.at[h, v], fw_recv.at[h, v], q_up[h])

        def lower(n):
            at = chunk(turn(q[h], -1), v, up + n, 16)
            g[at, cols[h]] = (scale * g[at, cols[h]].astype(F32)
                              + after[h] * r1[h, v, pl.ds(up + n, 16)].astype(F32)).astype(BF16)

        strips(piece - up, lower)
        remote(g.at[chunk(turn(q[h], -1), v, up, piece - up), cols[h]], fw.at[h, v, pl.ds(up, piece - up)],
               fw_send.at[h, v], fw_recv.at[h, v], q_down[h])

    upper_p, lower_p = pl.ds(0, cuts[0]), pl.ds(cuts[0], piece - cuts[0])

    def send_second(h, v):
        away = turn(v - r[h], 0)
        upper = g.at[chunk(q[h], v, 0, cuts[0]), cols[h]]
        lower = g.at[chunk(q[h], v, cuts[0], piece - cuts[0]), cols[h]]

        @pl.when(away == 1)
        def _():
            remote(lower, p2.at[h, lower_p], p_send.at[h], p2_recv.at[h], r_up[h])

        @pl.when(away == 2)
        def _():
            remote(upper, p1.at[h, upper_p], p_send.at[h], p1_recv.at[h], r_up[h])
            remote(lower, p1.at[h, lower_p], p_send.at[h], p1_recv.at[h], r_down[h])

        @pl.when(away == 3)
        def _():
            remote(upper, p2.at[h, upper_p], p_send.at[h], p2_recv.at[h], r_down[h])

    def gather_direct(h, v):
        await_bytes(g.at[pl.ds(0, 2 * piece), cols[h]], r2_recv.at[h, v])
        await_bytes(fw.at[h, v], fw_recv.at[h, v])

        def body(n):
            at, part = chunk(q[h], v, n, 16), pl.ds(n, 16)
            g[at, cols[h]] = (scale * g[at, cols[h]].astype(F32) + far[h] * fw[h, v, part].astype(F32)
                              + before[h] * from_down[h, v, part].astype(F32)
                              + after[h] * from_up[h, v, part].astype(F32)).astype(BF16)

        strips(piece, body)
        send_second(h, v)

    def gather_passed(h, v, up):
        await_bytes(g.at[pl.ds(0, piece), cols[h]], r2_recv.at[h, v])
        await_bytes(fw.at[h, v], fw_recv.at[h, v])

        def gathered(other, ref, start):
            def body(n):
                n = start + n
                at, part = chunk(q[h], v, n, 16), pl.ds(n, 16)
                g[at, cols[h]] = (scale * g[at, cols[h]].astype(F32) + fw[h, v, part].astype(F32)
                                  + other * ref[h, v, part].astype(F32)).astype(BF16)
            return body

        strips(up, gathered(after[h], from_up, 0))
        strips(piece - up, gathered(before[h], from_down, up))
        send_second(h, v)

    up, down = cuts[0], piece - cuts[0]

    def pass_second(h):
        await_bytes(p1.at[h], p1_recv.at[h])

        def upper(n):
            at = chunk(q[h], turn(r[h], 1), n, 16)
            g[at, cols[h]] = (g[at, cols[h]].astype(F32) + p1[h, pl.ds(n, 16)].astype(F32)).astype(BF16)

        strips(up, upper)
        remote(g.at[chunk(q[h], turn(r[h], 1), 0, up), cols[h]], pf.at[h, pl.ds(0, up)],
               p_send.at[h], pf_recv.at[h], r_up[h])

        def lower(n):
            at = chunk(q[h], turn(r[h], -1), up + n, 16)
            g[at, cols[h]] = (g[at, cols[h]].astype(F32) + p1[h, pl.ds(up + n, 16)].astype(F32)).astype(BF16)

        strips(down, lower)
        remote(g.at[chunk(q[h], turn(r[h], -1), up, down), cols[h]], pf.at[h, pl.ds(up, down)],
               p_send.at[h], pf_recv.at[h], r_down[h])

    @pl.loop(0, RING)
    def _(i):
        for h in range(2):
            v = turn(r[h], away_of(i))
            cut, direct = kind(h, v)
            for k in range(2):
                @pl.when((cut == k) & ~direct)
                def _():
                    pass_on(h, v, cuts[k])

    @pl.loop(0, RING)
    def _(i):
        @pl.when(i == RING - 1)
        def _():
            for h in range(2):
                pass_second(h)

        for h in range(2):
            v = turn(r[h], away_of(i))
            cut, direct = kind(h, v)

            @pl.when(direct)
            def _():
                gather_direct(h, v)

            for k in range(2):
                @pl.when((cut == k) & ~direct)
                def _():
                    gather_passed(h, v, cuts[k])

    def place(h, u, v, start=0, size=None):
        return out.at[chunk(u, v, start, size), cols[h]]

    def spread(h, away):
        v = turn(r[h], away)
        at = place(h, q[h], v)
        remote(at, at, ag2_send.at[h, away], ag2_recv.at[h, v, 0], q_up[h])
        remote(at, at, ag2_send.at[h, away], ag2_recv.at[h, v, 1], q_down[h])

    @pl.when(z != y)
    def _():
        await_bytes(nz_low.at[1], nz_recv)

    for h in range(2):
        await_bytes(p2.at[h], p2_recv.at[h])
        await_bytes(pf.at[h], pf_recv.at[h])

        def final(n):
            at = pl.ds(n, 16)
            whole = (g[chunk(q[h], r[h], n, 16), cols[h]].astype(F32) + p2[h, at].astype(F32)
                     + pf[h, at].astype(F32) + (nz_low[1, at].astype(F32) if h == 0 else nz[at, cols[1]]))
            out[chunk(q[h], r[h], n, 16), cols[h]] = (whole * (1.0 / 16.0)).astype(BF16)

        strips(piece, final)
        mine = place(h, q[h], r[h])
        remote(mine, mine, ag1_send.at[h], ag1_recv.at[h, 0], r_up[h])
        remote(mine, mine, ag1_send.at[h], ag1_recv.at[h, 1], r_down[h])
        spread(h, 0)

    for h in range(2):
        v = turn(r[h], -1)
        await_bytes(place(h, q[h], v), ag1_recv.at[h, 0])
        at = place(h, q[h], v, 0, up)
        remote(at, at, ag1_send.at[h], ag1_recv.at[h, 2], r_up[h])
        v = turn(r[h], 1)
        await_bytes(place(h, q[h], v), ag1_recv.at[h, 1])
        at = place(h, q[h], v, up, down)
        remote(at, at, ag1_send.at[h], ag1_recv.at[h, 2], r_down[h])
        spread(h, 3)
        spread(h, 1)

    def relay(h, away):
        v = turn(r[h], away)
        up = cuts[away % 2]
        u = turn(q[h], -1)
        await_bytes(place(h, u, v), ag2_recv.at[h, v, 0])
        at = place(h, u, v, 0, up)
        remote(at, at, ag2_send.at[h, away], ag2_recv.at[h, v, 2], q_up[h])
        u = turn(q[h], 1)
        await_bytes(place(h, u, v), ag2_recv.at[h, v, 1])
        at = place(h, u, v, up, piece - up)
        remote(at, at, ag2_send.at[h, away], ag2_recv.at[h, v, 2], q_down[h])

    for h in range(2):
        relay(h, 0)
    for h in range(2):
        v = turn(r[h], 2)
        await_bytes(place(h, q[h], v), ag1_recv.at[h, 2])
        spread(h, 2)
    for away in (3, 1, 2):
        for h in range(2):
            relay(h, away)
    for away in (0, 3, 1, 2):
        for h in range(2):
            v = turn(r[h], away)
            await_bytes(place(h, turn(q[h], 2), v), ag2_recv.at[h, v, 2])

    for h in range(2):
        await_bytes(g.at[pl.ds(0, 3 * piece), cols[0]], p_send.at[h])
        await_bytes(g.at[pl.ds(0, 3 * piece), cols[0]], ag1_send.at[h])
        for rel in range(RING):
            rows_out = (3 if rel in DIRECT[h] else 2) * piece
            await_bytes(g.at[pl.ds(0, rows_out), cols[0]], raw_send.at[h, second(h, rel)])
        for b in range(RING):
            await_bytes(g.at[pl.ds(0, piece), cols[0]], fw_send.at[h, b])
            await_bytes(g.at[pl.ds(0, 3 * piece), cols[0]], ag2_send.at[h, b])
    for side in range(2):
        for m in (4, 5):
            await_bytes(ot_v.at[pl.ds(0, piece)], x_send.at[side, m])
    @pl.when(z != y)
    def _():
        await_bytes(nz_low.at[0], nz_send)

    @pl.when(z == y)
    def _():
        await_bytes(nz_mid.at[pl.ds(0, 3)], mid_send)

    await_bytes(nrm.at[pl.ds(0, 7)], nrm_send)
    await_bytes(fac.at[pl.ds(1, 6)], fac_send)


def on_device(hidden, out_grad, lengths, noise):
    _, _, seq_len, units = hidden.shape
    block = out_grad.shape[3]
    width = block * lax.axis_size("tensor")
    layers = lax.axis_size("layer")
    bound = float((seq_len * layers * units * lax.axis_size("tensor") * width / 64.0) ** 0.5)
    piece, half = block // RING, units // 2
    dma = pltpu.SemaphoreType.DMA
    result = pl.pallas_call(
        functools.partial(kernel, bound),
        out_shape=pltpu.VMEM((width, units), BF16),
        in_specs=[pl.BlockSpec(memory_space=pltpu.SMEM)] + [pl.BlockSpec(memory_space=pltpu.HBM)] * 3,
        out_specs=pl.BlockSpec(memory_space=pltpu.VMEM),
        scratch_shapes=[
            pltpu.VMEM((seq_len, units), BF16),
            pltpu.VMEM((width, seq_len), BF16),
            pltpu.VMEM((width, units), BF16),
            pltpu.VMEM((2, RING, piece, half), BF16),
            pltpu.VMEM((2, RING, piece, half), BF16),
            pltpu.VMEM((2, RING, piece, half), BF16),
            pltpu.VMEM((2, RING, piece, half), BF16),
            pltpu.VMEM((2, piece, half), BF16),
            pltpu.VMEM((2, piece, half), BF16),
            pltpu.VMEM((2, piece, half), BF16),
            pltpu.VMEM((piece, units), F32),
            pltpu.VMEM((2, piece, half), BF16),
            pltpu.VMEM((RING, piece, half), BF16),
            pltpu.VMEM((8, half), F32),
            pltpu.VMEM((2 * RING, 8, 128), F32),
            pltpu.VMEM((7, 8, 128), F32),
            dma((3,)), dma((2, 6)), dma((2, 6)),
            dma((2, RING)), dma((2, RING)), dma((2, RING)), dma((2, RING)), dma((2, RING)),
            dma((2,)), dma((2,)), dma((2,)), dma((2,)),
            dma, dma, dma, dma, dma, dma, dma, dma,
            dma((2,)), dma((2, 3)), dma((2, RING)), dma((2, RING, 3)),
        ],
        compiler_params=pltpu.CompilerParams(
            collective_id=0, has_side_effects=True, vmem_limit_bytes=46 * 1024 * 1024
        ),
        cost_estimate=pl.CostEstimate(
            flops=2 * width * units * seq_len, bytes_accessed=30_000_000, transcendentals=0
        ),
    )(lengths, *(pltpu.with_memory_space_constraint(a, pltpu.HBM) for a in (out_grad[0, 0].T, hidden[0, 0], noise[0])))
    return result[None]


def solution(mesh):
    placed = (
        P("layer", "dp", None, "tensor"),
        P("layer", "dp", None, "tensor"),
        P("dp"),
        P("layer", "dp", "tensor"),
    )
    return jax.shard_map(
        on_device, mesh=mesh, in_specs=placed, out_specs=P("layer", None, "tensor"), check_vma=False
    )
```

```python
import functools

import jax
import jax.numpy as jnp
from jax import lax
from jax.experimental import pallas as pl
from jax.experimental.pallas import tpu as pltpu
from jax.sharding import PartitionSpec as P

MESH = pl.DeviceIdType.MESH
RING = 4
F32 = jnp.float32
DIRECT = ((0,), (0,))
BF16 = jnp.bfloat16


def kernel(bound, len_ref, o_hbm, h_hbm, noise_hbm, out,
           h_v, ot_v, g, r1, from_down, from_up, fw, p1, p2, pf, nz, nz_low, nz_mid, sq, nrm, fac,
           load_sem, x_send, x_recv, raw_send, r1_recv, r2_recv, fw_send, fw_recv,
           p_send, p1_recv, p2_recv, pf_recv, nz_send, nz_recv, mid_send, mid_recv, nrm_send, nrm_recv,
           fac_send, fac_recv, far_recv, ag1_send, ag1_recv, ag2_send, ag2_recv):
    dp = lax.axis_index("dp")
    x = lax.axis_index("tensor")
    core = lax.axis_index("layer")
    z, y = dp // RING, dp % RING
    block, tokens = o_hbm.shape
    units = h_hbm.shape[1]
    piece = block // RING
    half = units // 2
    cuts = (piece - piece // 32 * 16, piece // 32 * 16)

    def turn(i, by):
        return (i + by + RING) % RING

    z_up, z_down = {"dp": turn(z, 1) * RING + y}, {"dp": turn(z, -1) * RING + y}
    y_up, y_down = {"dp": z * RING + turn(y, 1)}, {"dp": z * RING + turn(y, -1)}
    x_up, x_down = {"tensor": turn(x, 1)}, {"tensor": turn(x, -1)}
    z_far, y_far = {"dp": turn(z, 2) * RING + y}, {"dp": z * RING + turn(y, 2)}
    q, r = (z, y), (y, z)
    q_up, q_down, q_far = (z_up, y_up), (z_down, y_down), (z_far, y_far)
    r_up, r_down = (y_up, z_up), (y_down, z_down)
    cols = (pl.ds(0, half), pl.ds(half, half))

    def rows(b, p, start=0, size=None):
        return pl.ds(pl.multiple_of(b * block + p * piece + start, 16), piece if size is None else size)

    def chunk(u, v, start=0, size=None):
        return rows(v, u, start, size)

    def remote(src, dst, send, recv, device):
        pltpu.make_async_remote_copy(src_ref=src, dst_ref=dst, send_sem=send, recv_sem=recv,
                                     device_id=device, device_id_type=MESH).start()

    def await_bytes(ref, sem):
        pltpu.make_async_copy(ref, ref, sem).wait()

    me = x * 2 + core
    group = []
    for k in range(1, 2 * RING):
        other = (me + k) % (2 * RING)
        group.append({"tensor": other // 2, "layer": other % 2})

    own = pl.multiple_of(x * block, 16)
    load_o = pltpu.make_async_copy(o_hbm, ot_v.at[pl.ds(own, block)], load_sem.at[1])
    load_o.start()
    load_h = pltpu.make_async_copy(h_hbm, h_v, load_sem.at[0])
    load_h.start()
    load_n = pltpu.make_async_copy(noise_hbm, nz, load_sem.at[2])
    load_n.start()

    barrier = pltpu.get_barrier_semaphore()
    for device in group + [z_up, z_down, z_far, y_up, y_down, y_far]:
        pl.semaphore_signal(barrier, inc=1, device_id=device, device_id_type=MESH)

    def passed_on(m):
        return m >= RING

    def first(m):
        return jnp.where((m == 0) | (m == 4), 0, jnp.where(m == 1, 2, jnp.where(m == 3, 3, 1)))

    def x_start(side, m, own, start=0, size=None):
        p = (first(m) + 2 * side) % RING
        device = (x_up, x_down)[side]
        if own:
            remote(o_hbm.at[pl.ds(pl.multiple_of(p * piece, 16), piece)], ot_v.at[rows(x, p)],
                   x_send.at[side, m], x_recv.at[side, m], device)
        else:
            at = ot_v.at[rows(turn(x, 2 * side - 1), p, start, size)]
            remote(at, at, x_send.at[side, m], x_recv.at[side, m], device)

    sq[...] = jnp.zeros_like(sq)
    pl.semaphore_wait(barrier, 13)
    for side in range(2):
        for m in range(2):
            x_start(side, jnp.int32(m), True)

    load_n.wait()

    @pl.loop(0, piece // 16)
    def _(n):
        at = pl.ds(pl.multiple_of(n * 16, 16), 16)
        low = nz[at, cols[0]].astype(BF16)
        nz_low[0, at] = low

        @pl.when(z == y)
        def _():
            nz_low[1, at] = low

    above, below = pl.ds(0, cuts[0]), pl.ds(cuts[0], piece - cuts[0])

    @pl.when(z != y)
    def _():
        remote(nz_low.at[0, above], nz_mid.at[z, above], nz_send, mid_recv, {"dp": y * RING + y})
        remote(nz_low.at[0, below], nz_mid.at[y, below], nz_send, mid_recv, {"dp": z * RING + z})

    load_h.wait()
    load_o.wait()

    @pl.loop(0, tokens // 16)
    def _(n):
        at = pl.ds(pl.multiple_of(n * 16, 16), 16)
        kept = n * 16 + lax.broadcasted_iota(jnp.int32, (16, units), 0) < len_ref[0]
        h_v[at] = jnp.where(kept, h_v[at], jnp.zeros((), BF16))

    def kind(h, b):
        ahead = turn(b - x, 0)
        direct = ahead == DIRECT[h][0]
        for rel in DIRECT[h][1:]:
            direct = direct | (ahead == rel)
        return ahead // 2, direct

    def send_raw(h, v, u):
        b, p = v, u
        away = turn(u - q[h], 0)
        cut, direct = kind(h, b)
        whole = g.at[rows(b, p), cols[h]]

        @pl.when(direct & (away == 1))
        def _():
            remote(whole, from_down.at[h, v], raw_send.at[h, v], r2_recv.at[h, v], q_up[h])

        @pl.when(direct & (away == 3))
        def _():
            remote(whole, from_up.at[h, v], raw_send.at[h, v], r2_recv.at[h, v], q_down[h])

        for k, up in enumerate(cuts):
            upper, lower = g.at[rows(b, p, 0, up), cols[h]], g.at[rows(b, p, up, piece - up), cols[h]]
            above, below = pl.ds(0, up), pl.ds(up, piece - up)

            @pl.when((cut == k) & ~direct & (away == 1))
            def _():
                remote(lower, from_down.at[h, v, below], raw_send.at[h, v], r2_recv.at[h, v], q_up[h])

            @pl.when((cut == k) & ~direct & (away == 3))
            def _():
                remote(upper, from_up.at[h, v, above], raw_send.at[h, v], r2_recv.at[h, v], q_down[h])

            @pl.when((cut == k) & (away == 2))
            def _():
                remote(upper, r1.at[h, v, above], raw_send.at[h, v], r1_recv.at[h, v], q_up[h])
                remote(lower, r1.at[h, v, below], raw_send.at[h, v], r1_recv.at[h, v], q_down[h])

    def product(ba, pa, bb, pb, start=0, size=piece):
        ra, rb = rows(ba, pa, start, size), rows(bb, pb, start, size)
        for h in range(2):
            left = jnp.concatenate([ot_v[ra], ot_v[rb]], axis=0)
            result = jnp.dot(left, h_v[:, cols[h]], preferred_element_type=F32)
            sq[...] += jnp.sum((result * result).reshape(2 * size // 8, 8, half), axis=0)
            low = result.astype(BF16)
            g[ra, cols[h]] = low[:size]
            g[rb, cols[h]] = low[size:]

    def send_all(*pieces):
        for b, p in pieces:
            for h in range(2):
                send_raw(h, b, p)

    def second(h, rel):
        return turn(x, rel)

    def relay_raw(h, rel):
        v = second(h, rel)
        up = cuts[rel // 2]
        await_bytes(r1.at[h, v], r1_recv.at[h, v])
        remote(r1.at[h, v, pl.ds(0, up)], fw.at[h, v, pl.ds(0, up)], fw_send.at[h, v], fw_recv.at[h, v], q_up[h])
        remote(r1.at[h, v, pl.ds(up, piece - up)], fw.at[h, v, pl.ds(up, piece - up)],
               fw_send.at[h, v], fw_recv.at[h, v], q_down[h])

    @pl.loop(0, 2)
    def _(i):
        product(x, 2 * i, x, 2 * i + 1)
        send_all((x, 2 * i), (x, 2 * i + 1))

    @pl.loop(0, 5)
    def _(i):
        ba, pa = jnp.where(passed_on(i), turn(x, 2), turn(x, -1)), first(i)
        bb, pb = jnp.where(passed_on(i), turn(x, 2), turn(x, 1)), (first(i) + 2) % RING
        await_bytes(ot_v.at[rows(ba, pa)], x_recv.at[0, i])
        await_bytes(ot_v.at[rows(bb, pb)], x_recv.at[1, i])

        @pl.when(i < 4)
        def _():
            await_bytes(ot_v.at[pl.ds(0, piece)], x_send.at[0, i])
            await_bytes(ot_v.at[pl.ds(0, piece)], x_send.at[1, i])

        for side in range(2):
            @pl.when(i + 2 < RING)
            def _():
                x_start(side, i + 2, True)

            @pl.when(i == 2)
            def _():
                x_start(side, i + 2, False)

            @pl.when(i == 3)
            def _():
                x_start(side, i + 2, False, 0, cuts[0])
                x_start(side, i + 3, False, cuts[0], cuts[1])

        product(ba, pa, bb, pb)

        send_all((ba, pa), (bb, pb))

        @pl.when((z == y) & (i == 1))
        def _():
            await_bytes(nz_mid.at[pl.ds(0, 3)], mid_recv)
            for k in range(1, RING):
                other = turn(z, k)
                remote(nz_mid.at[other, above], nz_low.at[1, above], mid_send, nz_recv, {"dp": z * RING + other})
                remote(nz_mid.at[other, below], nz_low.at[1, below], mid_send, nz_recv, {"dp": other * RING + z})


        @pl.when(i == 1)
        def _():
            for h in range(2):
                relay_raw(h, 0)

    far_block = turn(x, 2)
    for m, start, size in ((5, 0, cuts[0]), (6, cuts[0], cuts[1])):
        for side, p in enumerate((1, 3)):
            await_bytes(ot_v.at[rows(far_block, p, start, size)], x_recv.at[side, m])
        product(far_block, 1, far_block, 3, start, size)

    nrm[pl.ds(me, 1)] = sum(sq[:, k:k + 128] for k in range(0, half, 128))[None]
    for device in group:
        remote(nrm.at[me], nrm.at[me], nrm_send, nrm_recv, device)
    send_all((far_block, 1), (far_block, 3))

    for h in range(2):
        for rel in DIRECT[h][1:]:
            relay_raw(h, rel)

    await_bytes(nrm.at[pl.ds(0, 7)], nrm_recv)
    total = jnp.sum(jnp.sum(nrm[...], axis=0), keepdims=True)
    factor = jnp.minimum(jnp.float32(1.0), bound / jnp.sqrt(total + 1e-06))
    fac[0] = jnp.broadcast_to(factor, fac.shape[1:])
    for slot, device in ((1, z_up), (2, z_down), (3, y_up), (4, y_down)):
        remote(fac.at[0], fac.at[slot], fac_send, fac_recv, device)
    for slot, device in ((5, z_far), (6, y_far)):
        remote(fac.at[0], fac.at[slot], fac_send, far_recv, device)
    await_bytes(fac.at[pl.ds(1, 4)], fac_recv)
    scale = fac[0, 0:1, 0:1]
    before, after = ([fac[k + 2 * h, 0:1, 0:1] for h in range(2)] for k in (1, 2))

    def strips(size, body):
        @pl.loop(0, size // 16)
        def _(n):
            body(pl.multiple_of(n * 16, 16))

    def away_of(i):
        return jnp.where(i == 0, 2, jnp.where(i == 1, 1, jnp.where(i == 2, 3, 0)))

    def pass_on(h, v, up):
        await_bytes(r1.at[h, v], r1_recv.at[h, v])

        def upper(n):
            at = chunk(turn(q[h], 1), v, n, 16)
            g[at, cols[h]] = (scale * g[at, cols[h]].astype(F32)
                              + before[h] * r1[h, v, pl.ds(n, 16)].astype(F32)).astype(BF16)

        strips(up, upper)
        remote(g.at[chunk(turn(q[h], 1), v, 0, up), cols[h]], fw.at[h, v, pl.ds(0, up)],
               fw_send.at[h, v], fw_recv.at[h, v], q_up[h])

        def lower(n):
            at = chunk(turn(q[h], -1), v, up + n, 16)
            g[at, cols[h]] = (scale * g[at, cols[h]].astype(F32)
                              + after[h] * r1[h, v, pl.ds(up + n, 16)].astype(F32)).astype(BF16)

        strips(piece - up, lower)
        remote(g.at[chunk(turn(q[h], -1), v, up, piece - up), cols[h]], fw.at[h, v, pl.ds(up, piece - up)],
               fw_send.at[h, v], fw_recv.at[h, v], q_down[h])

    upper_p, lower_p = pl.ds(0, cuts[0]), pl.ds(cuts[0], piece - cuts[0])

    def send_second(h, v):
        away = turn(v - r[h], 0)
        upper = g.at[chunk(q[h], v, 0, cuts[0]), cols[h]]
        lower = g.at[chunk(q[h], v, cuts[0], piece - cuts[0]), cols[h]]

        @pl.when(away == 1)
        def _():
            remote(lower, p2.at[h, lower_p], p_send.at[h], p2_recv.at[h], r_up[h])

        @pl.when(away == 2)
        def _():
            remote(upper, p1.at[h, upper_p], p_send.at[h], p1_recv.at[h], r_up[h])
            remote(lower, p1.at[h, lower_p], p_send.at[h], p1_recv.at[h], r_down[h])

        @pl.when(away == 3)
        def _():
            remote(upper, p2.at[h, upper_p], p_send.at[h], p2_recv.at[h], r_down[h])

    def gather_direct(h, v):
        await_bytes(g.at[pl.ds(0, 2 * piece), cols[h]], r2_recv.at[h, v])
        await_bytes(fw.at[h, v], fw_recv.at[h, v])

        def body(n):
            at, part = chunk(q[h], v, n, 16), pl.ds(n, 16)
            g[at, cols[h]] = (scale * g[at, cols[h]].astype(F32) + far[h] * fw[h, v, part].astype(F32)
                              + before[h] * from_down[h, v, part].astype(F32)
                              + after[h] * from_up[h, v, part].astype(F32)).astype(BF16)

        strips(piece, body)
        send_second(h, v)

    def gather_passed(h, v, up):
        await_bytes(g.at[pl.ds(0, piece), cols[h]], r2_recv.at[h, v])
        await_bytes(fw.at[h, v], fw_recv.at[h, v])

        def gathered(other, ref, start):
            def body(n):
                n = start + n
                at, part = chunk(q[h], v, n, 16), pl.ds(n, 16)
                g[at, cols[h]] = (scale * g[at, cols[h]].astype(F32) + fw[h, v, part].astype(F32)
                                  + other * ref[h, v, part].astype(F32)).astype(BF16)
            return body

        strips(up, gathered(after[h], from_up, 0))
        strips(piece - up, gathered(before[h], from_down, up))
        send_second(h, v)

    up, down = cuts[0], piece - cuts[0]

    def pass_second(h):
        await_bytes(p1.at[h], p1_recv.at[h])

        def upper(n):
            at = chunk(q[h], turn(r[h], 1), n, 16)
            g[at, cols[h]] = (g[at, cols[h]].astype(F32) + p1[h, pl.ds(n, 16)].astype(F32)).astype(BF16)

        strips(up, upper)
        remote(g.at[chunk(q[h], turn(r[h], 1), 0, up), cols[h]], pf.at[h, pl.ds(0, up)],
               p_send.at[h], pf_recv.at[h], r_up[h])

        def lower(n):
            at = chunk(q[h], turn(r[h], -1), up + n, 16)
            g[at, cols[h]] = (g[at, cols[h]].astype(F32) + p1[h, pl.ds(up + n, 16)].astype(F32)).astype(BF16)

        strips(down, lower)
        remote(g.at[chunk(q[h], turn(r[h], -1), up, down), cols[h]], pf.at[h, pl.ds(up, down)],
               p_send.at[h], pf_recv.at[h], r_down[h])

    @pl.loop(0, RING)
    def _(i):
        for h in range(2):
            v = turn(r[h], away_of(i))
            cut, direct = kind(h, v)
            for k in range(2):
                @pl.when((cut == k) & ~direct)
                def _():
                    pass_on(h, v, cuts[k])

    await_bytes(fac.at[pl.ds(5, 2)], far_recv)
    far = [fac[5 + h, 0:1, 0:1] for h in range(2)]

    @pl.loop(0, RING)
    def _(i):
        @pl.when(i == RING - 1)
        def _():
            for h in range(2):
                pass_second(h)

        for h in range(2):
            v = turn(r[h], away_of(i))
            cut, direct = kind(h, v)

            @pl.when(direct)
            def _():
                gather_direct(h, v)

            for k in range(2):
                @pl.when((cut == k) & ~direct)
                def _():
                    gather_passed(h, v, cuts[k])

    def place(h, u, v, start=0, size=None):
        return out.at[chunk(u, v, start, size), cols[h]]

    def spread(h, away):
        v = turn(r[h], away)
        at = place(h, q[h], v)
        remote(at, at, ag2_send.at[h, away], ag2_recv.at[h, v, 0], q_up[h])
        remote(at, at, ag2_send.at[h, away], ag2_recv.at[h, v, 1], q_down[h])

    @pl.when(z != y)
    def _():
        await_bytes(nz_low.at[1], nz_recv)

    for h in range(2):
        await_bytes(p2.at[h], p2_recv.at[h])
        await_bytes(pf.at[h], pf_recv.at[h])

        def final(n):
            at = pl.ds(n, 16)
            whole = (g[chunk(q[h], r[h], n, 16), cols[h]].astype(F32) + p2[h, at].astype(F32)
                     + pf[h, at].astype(F32) + (nz_low[1, at].astype(F32) if h == 0 else nz[at, cols[1]]))
            out[chunk(q[h], r[h], n, 16), cols[h]] = (whole * (1.0 / 16.0)).astype(BF16)

        strips(piece, final)
        mine = place(h, q[h], r[h])
        remote(mine, mine, ag1_send.at[h], ag1_recv.at[h, 0], r_up[h])
        remote(mine, mine, ag1_send.at[h], ag1_recv.at[h, 1], r_down[h])
        spread(h, 0)

    for h in range(2):
        v = turn(r[h], -1)
        await_bytes(place(h, q[h], v), ag1_recv.at[h, 0])
        at = place(h, q[h], v, 0, up)
        remote(at, at, ag1_send.at[h], ag1_recv.at[h, 2], r_up[h])
        v = turn(r[h], 1)
        await_bytes(place(h, q[h], v), ag1_recv.at[h, 1])
        at = place(h, q[h], v, up, down)
        remote(at, at, ag1_send.at[h], ag1_recv.at[h, 2], r_down[h])
        spread(h, 3)
        spread(h, 1)

    def relay(h, away):
        v = turn(r[h], away)
        up = cuts[away % 2]
        u = turn(q[h], -1)
        await_bytes(place(h, u, v), ag2_recv.at[h, v, 0])
        at = place(h, u, v, 0, up)
        remote(at, at, ag2_send.at[h, away], ag2_recv.at[h, v, 2], q_up[h])
        u = turn(q[h], 1)
        await_bytes(place(h, u, v), ag2_recv.at[h, v, 1])
        at = place(h, u, v, up, piece - up)
        remote(at, at, ag2_send.at[h, away], ag2_recv.at[h, v, 2], q_down[h])

    for h in range(2):
        relay(h, 0)
    for h in range(2):
        v = turn(r[h], 2)
        await_bytes(place(h, q[h], v), ag1_recv.at[h, 2])
        spread(h, 2)
    for away in (3, 1, 2):
        for h in range(2):
            relay(h, away)
    for away in (0, 3, 1, 2):
        for h in range(2):
            v = turn(r[h], away)
            await_bytes(place(h, turn(q[h], 2), v), ag2_recv.at[h, v, 2])

    for h in range(2):
        await_bytes(g.at[pl.ds(0, 3 * piece), cols[0]], p_send.at[h])
        await_bytes(g.at[pl.ds(0, 3 * piece), cols[0]], ag1_send.at[h])
        for rel in range(RING):
            rows_out = (3 if rel in DIRECT[h] else 2) * piece
            await_bytes(g.at[pl.ds(0, rows_out), cols[0]], raw_send.at[h, second(h, rel)])
        for b in range(RING):
            await_bytes(g.at[pl.ds(0, piece), cols[0]], fw_send.at[h, b])
            await_bytes(g.at[pl.ds(0, 3 * piece), cols[0]], ag2_send.at[h, b])
    for side in range(2):
        for m, size in ((4, piece), (5, cuts[0]), (6, cuts[1])):
            await_bytes(ot_v.at[pl.ds(0, size)], x_send.at[side, m])
    @pl.when(z != y)
    def _():
        await_bytes(nz_low.at[0], nz_send)

    @pl.when(z == y)
    def _():
        await_bytes(nz_mid.at[pl.ds(0, 3)], mid_send)

    await_bytes(nrm.at[pl.ds(0, 7)], nrm_send)
    await_bytes(fac.at[pl.ds(1, 6)], fac_send)


def on_device(hidden, out_grad, lengths, noise):
    _, _, seq_len, units = hidden.shape
    block = out_grad.shape[3]
    width = block * lax.axis_size("tensor")
    layers = lax.axis_size("layer")
    bound = float((seq_len * layers * units * lax.axis_size("tensor") * width / 64.0) ** 0.5)
    piece, half = block // RING, units // 2
    dma = pltpu.SemaphoreType.DMA
    result = pl.pallas_call(
        functools.partial(kernel, bound),
        out_shape=pltpu.VMEM((width, units), BF16),
        in_specs=[pl.BlockSpec(memory_space=pltpu.SMEM)] + [pl.BlockSpec(memory_space=pltpu.HBM)] * 3,
        out_specs=pl.BlockSpec(memory_space=pltpu.VMEM),
        scratch_shapes=[
            pltpu.VMEM((seq_len, units), BF16),
            pltpu.VMEM((width, seq_len), BF16),
            pltpu.VMEM((width, units), BF16),
            pltpu.VMEM((2, RING, piece, half), BF16),
            pltpu.VMEM((2, RING, piece, half), BF16),
            pltpu.VMEM((2, RING, piece, half), BF16),
            pltpu.VMEM((2, RING, piece, half), BF16),
            pltpu.VMEM((2, piece, half), BF16),
            pltpu.VMEM((2, piece, half), BF16),
            pltpu.VMEM((2, piece, half), BF16),
            pltpu.VMEM((piece, units), F32),
            pltpu.VMEM((2, piece, half), BF16),
            pltpu.VMEM((RING, piece, half), BF16),
            pltpu.VMEM((8, half), F32),
            pltpu.VMEM((2 * RING, 8, 128), F32),
            pltpu.VMEM((7, 8, 128), F32),
            dma((3,)), dma((2, 7)), dma((2, 7)),
            dma((2, RING)), dma((2, RING)), dma((2, RING)), dma((2, RING)), dma((2, RING)),
            dma((2,)), dma((2,)), dma((2,)), dma((2,)),
            dma, dma, dma, dma, dma, dma, dma, dma, dma,
            dma((2,)), dma((2, 3)), dma((2, RING)), dma((2, RING, 3)),
        ],
        compiler_params=pltpu.CompilerParams(
            collective_id=0, has_side_effects=True, vmem_limit_bytes=46 * 1024 * 1024
        ),
        cost_estimate=pl.CostEstimate(
            flops=2 * width * units * seq_len, bytes_accessed=30_000_000, transcendentals=0
        ),
    )(lengths, *(pltpu.with_memory_space_constraint(a, pltpu.HBM) for a in (out_grad[0, 0].T, hidden[0, 0], noise[0])))
    return result[None]


def solution(mesh):
    placed = (
        P("layer", "dp", None, "tensor"),
        P("layer", "dp", None, "tensor"),
        P("dp"),
        P("layer", "dp", "tensor"),
    )
    return jax.shard_map(
        on_device, mesh=mesh, in_specs=placed, out_specs=P("layer", None, "tensor"), check_vma=False
    )
```

```python
import functools

import jax
import jax.numpy as jnp
from jax import lax
from jax.experimental import pallas as pl
from jax.experimental.pallas import tpu as pltpu
from jax.sharding import PartitionSpec as P

MESH = pl.DeviceIdType.MESH
RING = 4
F32 = jnp.float32
DIRECT = ((0,), (0,))
BF16 = jnp.bfloat16


def kernel(bound, len_ref, o_hbm, h_hbm, noise_hbm, out,
           h_v, ot_v, g, r1, from_down, from_up, fw, p1, p2, pf, nz, nz_low, nz_mid, sq, nrm, fac,
           load_sem, x_send, x_recv, raw_send, r1_recv, r2_recv, fw_send, fw_recv,
           p_send, p1_recv, p2_recv, pf_recv, nz_send, nz_recv, mid_send, mid_recv, nrm_send, nrm_recv,
           fac_send, fac_recv, far_recv, ag1_send, ag1_recv, ag2_send, ag2_recv):
    dp = lax.axis_index("dp")
    x = lax.axis_index("tensor")
    core = lax.axis_index("layer")
    z, y = dp // RING, dp % RING
    block, tokens = o_hbm.shape
    units = h_hbm.shape[1]
    piece = block // RING
    half = units // 2
    cuts = (piece - piece // 32 * 16, piece // 32 * 16)

    def turn(i, by):
        return (i + by + RING) % RING

    z_up, z_down = {"dp": turn(z, 1) * RING + y}, {"dp": turn(z, -1) * RING + y}
    y_up, y_down = {"dp": z * RING + turn(y, 1)}, {"dp": z * RING + turn(y, -1)}
    x_up, x_down = {"tensor": turn(x, 1)}, {"tensor": turn(x, -1)}
    z_far, y_far = {"dp": turn(z, 2) * RING + y}, {"dp": z * RING + turn(y, 2)}
    q, r = (z, y), (y, z)
    q_up, q_down, q_far = (z_up, y_up), (z_down, y_down), (z_far, y_far)
    r_up, r_down = (y_up, z_up), (y_down, z_down)
    cols = (pl.ds(0, half), pl.ds(half, half))

    def rows(b, p, start=0, size=None):
        return pl.ds(pl.multiple_of(b * block + p * piece + start, 16), piece if size is None else size)

    def chunk(u, v, start=0, size=None):
        return rows(v, u, start, size)

    def remote(src, dst, send, recv, device):
        pltpu.make_async_remote_copy(src_ref=src, dst_ref=dst, send_sem=send, recv_sem=recv,
                                     device_id=device, device_id_type=MESH).start()

    def await_bytes(ref, sem):
        pltpu.make_async_copy(ref, ref, sem).wait()

    me = x * 2 + core
    group = []
    for k in range(1, 2 * RING):
        other = (me + k) % (2 * RING)
        group.append({"tensor": other // 2, "layer": other % 2})

    barrier = pltpu.get_barrier_semaphore()
    for device in group + [z_up, z_down, z_far, y_up, y_down, y_far]:
        pl.semaphore_signal(barrier, inc=1, device_id=device, device_id_type=MESH)

    own = pl.multiple_of(x * block, 16)
    load_o = pltpu.make_async_copy(o_hbm, ot_v.at[pl.ds(own, block)], load_sem.at[1])
    load_o.start()
    load_h = pltpu.make_async_copy(h_hbm, h_v, load_sem.at[0])
    load_h.start()
    load_n = pltpu.make_async_copy(noise_hbm, nz, load_sem.at[2])
    load_n.start()

    def passed_on(m):
        return m >= RING

    def first(m):
        return jnp.where((m == 0) | (m == 4), 0, jnp.where(m == 1, 2, jnp.where(m == 3, 3, 1)))

    def x_start(side, m, own, start=0, size=None):
        p = (first(m) + 2 * side) % RING
        device = (x_up, x_down)[side]
        if own:
            remote(o_hbm.at[pl.ds(pl.multiple_of(p * piece, 16), piece)], ot_v.at[rows(x, p)],
                   x_send.at[side, m], x_recv.at[side, m], device)
        else:
            at = ot_v.at[rows(turn(x, 2 * side - 1), p, start, size)]
            remote(at, at, x_send.at[side, m], x_recv.at[side, m], device)

    sq[...] = jnp.zeros_like(sq)
    pl.semaphore_wait(barrier, 13)
    for side in range(2):
        for m in range(2):
            x_start(side, jnp.int32(m), True)

    load_n.wait()

    @pl.loop(0, piece // 16)
    def _(n):
        at = pl.ds(pl.multiple_of(n * 16, 16), 16)
        low = nz[at, cols[0]].astype(BF16)
        nz_low[0, at] = low

        @pl.when(z == y)
        def _():
            nz_low[1, at] = low

    above, below = pl.ds(0, cuts[0]), pl.ds(cuts[0], piece - cuts[0])

    @pl.when(z != y)
    def _():
        remote(nz_low.at[0, above], nz_mid.at[z, above], nz_send, mid_recv, {"dp": y * RING + y})
        remote(nz_low.at[0, below], nz_mid.at[y, below], nz_send, mid_recv, {"dp": z * RING + z})

    load_h.wait()
    load_o.wait()

    @pl.loop(0, tokens // 16)
    def _(n):
        at = pl.ds(pl.multiple_of(n * 16, 16), 16)
        kept = n * 16 + lax.broadcasted_iota(jnp.int32, (16, units), 0) < len_ref[0]
        h_v[at] = jnp.where(kept, h_v[at], jnp.zeros((), BF16))

    def kind(h, b):
        ahead = turn(b - x, 0)
        direct = ahead == DIRECT[h][0]
        for rel in DIRECT[h][1:]:
            direct = direct | (ahead == rel)
        return ahead // 2, direct

    def send_raw(h, v, u):
        b, p = v, u
        away = turn(u - q[h], 0)
        cut, direct = kind(h, b)
        whole = g.at[rows(b, p), cols[h]]

        @pl.when(direct & (away == 1))
        def _():
            remote(whole, from_down.at[h, v], raw_send.at[h, v], r2_recv.at[h, v], q_up[h])

        @pl.when(direct & (away == 3))
        def _():
            remote(whole, from_up.at[h, v], raw_send.at[h, v], r2_recv.at[h, v], q_down[h])

        for k, up in enumerate(cuts):
            upper, lower = g.at[rows(b, p, 0, up), cols[h]], g.at[rows(b, p, up, piece - up), cols[h]]
            above, below = pl.ds(0, up), pl.ds(up, piece - up)

            @pl.when((cut == k) & ~direct & (away == 1))
            def _():
                remote(lower, from_down.at[h, v, below], raw_send.at[h, v], r2_recv.at[h, v], q_up[h])

            @pl.when((cut == k) & ~direct & (away == 3))
            def _():
                remote(upper, from_up.at[h, v, above], raw_send.at[h, v], r2_recv.at[h, v], q_down[h])

            @pl.when((cut == k) & (away == 2))
            def _():
                remote(upper, r1.at[h, v, above], raw_send.at[h, v], r1_recv.at[h, v], q_up[h])
                remote(lower, r1.at[h, v, below], raw_send.at[h, v], r1_recv.at[h, v], q_down[h])

    def product(ba, pa, bb, pb, start=0, size=piece):
        ra, rb = rows(ba, pa, start, size), rows(bb, pb, start, size)
        for h in range(2):
            left = jnp.concatenate([ot_v[ra], ot_v[rb]], axis=0)
            result = jnp.dot(left, h_v[:, cols[h]], preferred_element_type=F32)
            sq[...] += jnp.sum((result * result).reshape(2 * size // 8, 8, half), axis=0)
            low = result.astype(BF16)
            g[ra, cols[h]] = low[:size]
            g[rb, cols[h]] = low[size:]

    def send_all(*pieces):
        for b, p in pieces:
            for h in range(2):
                send_raw(h, b, p)

    def second(h, rel):
        return turn(x, rel)

    def relay_raw(h, rel):
        v = second(h, rel)
        up = cuts[rel // 2]
        await_bytes(r1.at[h, v], r1_recv.at[h, v])
        remote(r1.at[h, v, pl.ds(0, up)], fw.at[h, v, pl.ds(0, up)], fw_send.at[h, v], fw_recv.at[h, v], q_up[h])
        remote(r1.at[h, v, pl.ds(up, piece - up)], fw.at[h, v, pl.ds(up, piece - up)],
               fw_send.at[h, v], fw_recv.at[h, v], q_down[h])

    @pl.loop(0, 2)
    def _(i):
        product(x, 2 * i, x, 2 * i + 1)
        send_all((x, 2 * i), (x, 2 * i + 1))

    @pl.loop(0, 5)
    def _(i):
        ba, pa = jnp.where(passed_on(i), turn(x, 2), turn(x, -1)), first(i)
        bb, pb = jnp.where(passed_on(i), turn(x, 2), turn(x, 1)), (first(i) + 2) % RING
        await_bytes(ot_v.at[rows(ba, pa)], x_recv.at[0, i])
        await_bytes(ot_v.at[rows(bb, pb)], x_recv.at[1, i])

        @pl.when(i < 4)
        def _():
            await_bytes(ot_v.at[pl.ds(0, piece)], x_send.at[0, i])
            await_bytes(ot_v.at[pl.ds(0, piece)], x_send.at[1, i])

        for side in range(2):
            @pl.when(i + 2 < RING)
            def _():
                x_start(side, i + 2, True)

            @pl.when(i == 2)
            def _():
                x_start(side, i + 2, False)

            @pl.when(i == 3)
            def _():
                x_start(side, i + 2, False, 0, cuts[0])
                x_start(side, i + 3, False, cuts[0], cuts[1])

        product(ba, pa, bb, pb)

        send_all((ba, pa), (bb, pb))

        @pl.when((z == y) & (i == 1))
        def _():
            await_bytes(nz_mid.at[pl.ds(0, 3)], mid_recv)
            for k in range(1, RING):
                other = turn(z, k)
                remote(nz_mid.at[other, above], nz_low.at[1, above], mid_send, nz_recv, {"dp": z * RING + other})
                remote(nz_mid.at[other, below], nz_low.at[1, below], mid_send, nz_recv, {"dp": other * RING + z})


        @pl.when(i == 1)
        def _():
            for h in range(2):
                relay_raw(h, 0)

    far_block = turn(x, 2)
    for m, start, size in ((5, 0, cuts[0]), (6, cuts[0], cuts[1])):
        for side, p in enumerate((1, 3)):
            await_bytes(ot_v.at[rows(far_block, p, start, size)], x_recv.at[side, m])
        product(far_block, 1, far_block, 3, start, size)

    nrm[pl.ds(me, 1)] = sum(sq[:, k:k + 128] for k in range(0, half, 128))[None]
    for device in group:
        remote(nrm.at[me], nrm.at[me], nrm_send, nrm_recv, device)
    send_all((far_block, 1), (far_block, 3))

    for h in range(2):
        for rel in DIRECT[h][1:]:
            relay_raw(h, rel)

    await_bytes(nrm.at[pl.ds(0, 7)], nrm_recv)
    total = jnp.sum(jnp.sum(nrm[...], axis=0), keepdims=True)
    factor = jnp.minimum(jnp.float32(1.0), bound / jnp.sqrt(total + 1e-06))
    fac[0] = jnp.broadcast_to(factor, fac.shape[1:])
    for slot, device in ((1, z_up), (2, z_down), (3, y_up), (4, y_down)):
        remote(fac.at[0], fac.at[slot], fac_send, fac_recv, device)
    for slot, device in ((5, z_far), (6, y_far)):
        remote(fac.at[0], fac.at[slot], fac_send, far_recv, device)
    await_bytes(fac.at[pl.ds(1, 4)], fac_recv)
    scale = fac[0, 0:1, 0:1]
    before, after = ([fac[k + 2 * h, 0:1, 0:1] for h in range(2)] for k in (1, 2))

    def strips(size, body):
        @pl.loop(0, size // 16)
        def _(n):
            body(pl.multiple_of(n * 16, 16))

    def away_of(i):
        return jnp.where(i == 0, 2, jnp.where(i == 1, 1, jnp.where(i == 2, 3, 0)))

    def pass_on(h, v, up):
        await_bytes(r1.at[h, v], r1_recv.at[h, v])

        def upper(n):
            at = chunk(turn(q[h], 1), v, n, 16)
            g[at, cols[h]] = (scale * g[at, cols[h]].astype(F32)
                              + before[h] * r1[h, v, pl.ds(n, 16)].astype(F32)).astype(BF16)

        strips(up, upper)
        remote(g.at[chunk(turn(q[h], 1), v, 0, up), cols[h]], fw.at[h, v, pl.ds(0, up)],
               fw_send.at[h, v], fw_recv.at[h, v], q_up[h])

        def lower(n):
            at = chunk(turn(q[h], -1), v, up + n, 16)
            g[at, cols[h]] = (scale * g[at, cols[h]].astype(F32)
                              + after[h] * r1[h, v, pl.ds(up + n, 16)].astype(F32)).astype(BF16)

        strips(piece - up, lower)
        remote(g.at[chunk(turn(q[h], -1), v, up, piece - up), cols[h]], fw.at[h, v, pl.ds(up, piece - up)],
               fw_send.at[h, v], fw_recv.at[h, v], q_down[h])

    upper_p, lower_p = pl.ds(0, cuts[0]), pl.ds(cuts[0], piece - cuts[0])

    def send_second(h, v):
        away = turn(v - r[h], 0)
        upper = g.at[chunk(q[h], v, 0, cuts[0]), cols[h]]
        lower = g.at[chunk(q[h], v, cuts[0], piece - cuts[0]), cols[h]]

        @pl.when(away == 1)
        def _():
            remote(lower, p2.at[h, lower_p], p_send.at[h], p2_recv.at[h], r_up[h])

        @pl.when(away == 2)
        def _():
            remote(upper, p1.at[h, upper_p], p_send.at[h], p1_recv.at[h], r_up[h])
            remote(lower, p1.at[h, lower_p], p_send.at[h], p1_recv.at[h], r_down[h])

        @pl.when(away == 3)
        def _():
            remote(upper, p2.at[h, upper_p], p_send.at[h], p2_recv.at[h], r_down[h])

    def gather_direct(h, v):
        await_bytes(g.at[pl.ds(0, 2 * piece), cols[h]], r2_recv.at[h, v])
        await_bytes(fw.at[h, v], fw_recv.at[h, v])

        def body(n):
            at, part = chunk(q[h], v, n, 16), pl.ds(n, 16)
            g[at, cols[h]] = (scale * g[at, cols[h]].astype(F32) + far[h] * fw[h, v, part].astype(F32)
                              + before[h] * from_down[h, v, part].astype(F32)
                              + after[h] * from_up[h, v, part].astype(F32)).astype(BF16)

        strips(piece, body)
        send_second(h, v)

    def gather_passed(h, v, up):
        await_bytes(g.at[pl.ds(0, piece), cols[h]], r2_recv.at[h, v])
        await_bytes(fw.at[h, v], fw_recv.at[h, v])

        def gathered(other, ref, start):
            def body(n):
                n = start + n
                at, part = chunk(q[h], v, n, 16), pl.ds(n, 16)
                g[at, cols[h]] = (scale * g[at, cols[h]].astype(F32) + fw[h, v, part].astype(F32)
                                  + other * ref[h, v, part].astype(F32)).astype(BF16)
            return body

        strips(up, gathered(after[h], from_up, 0))
        strips(piece - up, gathered(before[h], from_down, up))
        send_second(h, v)

    up, down = cuts[0], piece - cuts[0]

    def pass_second(h):
        await_bytes(p1.at[h], p1_recv.at[h])

        def upper(n):
            at = chunk(q[h], turn(r[h], 1), n, 16)
            g[at, cols[h]] = (g[at, cols[h]].astype(F32) + p1[h, pl.ds(n, 16)].astype(F32)).astype(BF16)

        strips(up, upper)
        remote(g.at[chunk(q[h], turn(r[h], 1), 0, up), cols[h]], pf.at[h, pl.ds(0, up)],
               p_send.at[h], pf_recv.at[h], r_up[h])

        def lower(n):
            at = chunk(q[h], turn(r[h], -1), up + n, 16)
            g[at, cols[h]] = (g[at, cols[h]].astype(F32) + p1[h, pl.ds(up + n, 16)].astype(F32)).astype(BF16)

        strips(down, lower)
        remote(g.at[chunk(q[h], turn(r[h], -1), up, down), cols[h]], pf.at[h, pl.ds(up, down)],
               p_send.at[h], pf_recv.at[h], r_down[h])

    @pl.loop(0, RING)
    def _(i):
        for h in range(2):
            v = turn(r[h], away_of(i))
            cut, direct = kind(h, v)
            for k in range(2):
                @pl.when((cut == k) & ~direct)
                def _():
                    pass_on(h, v, cuts[k])

    await_bytes(fac.at[pl.ds(5, 2)], far_recv)
    far = [fac[5 + h, 0:1, 0:1] for h in range(2)]

    @pl.loop(0, RING)
    def _(i):
        @pl.when(i == RING - 1)
        def _():
            for h in range(2):
                pass_second(h)

        for h in range(2):
            v = turn(r[h], away_of(i))
            cut, direct = kind(h, v)

            @pl.when(direct)
            def _():
                gather_direct(h, v)

            for k in range(2):
                @pl.when((cut == k) & ~direct)
                def _():
                    gather_passed(h, v, cuts[k])

    def place(h, u, v, start=0, size=None):
        return out.at[chunk(u, v, start, size), cols[h]]

    def spread(h, away):
        v = turn(r[h], away)
        at = place(h, q[h], v)
        remote(at, at, ag2_send.at[h, away], ag2_recv.at[h, v, 0], q_up[h])
        remote(at, at, ag2_send.at[h, away], ag2_recv.at[h, v, 1], q_down[h])

    @pl.when(z != y)
    def _():
        await_bytes(nz_low.at[1], nz_recv)

    for h in range(2):
        await_bytes(p2.at[h], p2_recv.at[h])
        await_bytes(pf.at[h], pf_recv.at[h])

        def final(n):
            at = pl.ds(n, 16)
            whole = (g[chunk(q[h], r[h], n, 16), cols[h]].astype(F32) + p2[h, at].astype(F32)
                     + pf[h, at].astype(F32) + (nz_low[1, at].astype(F32) if h == 0 else nz[at, cols[1]]))
            out[chunk(q[h], r[h], n, 16), cols[h]] = (whole * (1.0 / 16.0)).astype(BF16)

        strips(piece, final)
        mine = place(h, q[h], r[h])
        remote(mine, mine, ag1_send.at[h], ag1_recv.at[h, 0], r_up[h])
        remote(mine, mine, ag1_send.at[h], ag1_recv.at[h, 1], r_down[h])
        spread(h, 0)

    for h in range(2):
        v = turn(r[h], -1)
        await_bytes(place(h, q[h], v), ag1_recv.at[h, 0])
        at = place(h, q[h], v, 0, up)
        remote(at, at, ag1_send.at[h], ag1_recv.at[h, 2], r_up[h])
        v = turn(r[h], 1)
        await_bytes(place(h, q[h], v), ag1_recv.at[h, 1])
        at = place(h, q[h], v, up, down)
        remote(at, at, ag1_send.at[h], ag1_recv.at[h, 2], r_down[h])
        spread(h, 3)
        spread(h, 1)

    def relay(h, away):
        v = turn(r[h], away)
        up = cuts[away % 2]
        u = turn(q[h], -1)
        await_bytes(place(h, u, v), ag2_recv.at[h, v, 0])
        at = place(h, u, v, 0, up)
        remote(at, at, ag2_send.at[h, away], ag2_recv.at[h, v, 2], q_up[h])
        u = turn(q[h], 1)
        await_bytes(place(h, u, v), ag2_recv.at[h, v, 1])
        at = place(h, u, v, up, piece - up)
        remote(at, at, ag2_send.at[h, away], ag2_recv.at[h, v, 2], q_down[h])

    for h in range(2):
        relay(h, 0)
    for h in range(2):
        v = turn(r[h], 2)
        await_bytes(place(h, q[h], v), ag1_recv.at[h, 2])
        spread(h, 2)
    for away in (3, 1, 2):
        for h in range(2):
            relay(h, away)
    for away in (0, 3, 1, 2):
        for h in range(2):
            v = turn(r[h], away)
            await_bytes(place(h, turn(q[h], 2), v), ag2_recv.at[h, v, 2])

    for h in range(2):
        await_bytes(g.at[pl.ds(0, 3 * piece), cols[0]], p_send.at[h])
        await_bytes(g.at[pl.ds(0, 3 * piece), cols[0]], ag1_send.at[h])
        for rel in range(RING):
            rows_out = (3 if rel in DIRECT[h] else 2) * piece
            await_bytes(g.at[pl.ds(0, rows_out), cols[0]], raw_send.at[h, second(h, rel)])
        for b in range(RING):
            await_bytes(g.at[pl.ds(0, piece), cols[0]], fw_send.at[h, b])
            await_bytes(g.at[pl.ds(0, 3 * piece), cols[0]], ag2_send.at[h, b])
    for side in range(2):
        for m, size in ((4, piece), (5, cuts[0]), (6, cuts[1])):
            await_bytes(ot_v.at[pl.ds(0, size)], x_send.at[side, m])
    @pl.when(z != y)
    def _():
        await_bytes(nz_low.at[0], nz_send)

    @pl.when(z == y)
    def _():
        await_bytes(nz_mid.at[pl.ds(0, 3)], mid_send)

    await_bytes(nrm.at[pl.ds(0, 7)], nrm_send)
    await_bytes(fac.at[pl.ds(1, 6)], fac_send)


def on_device(hidden, out_grad, lengths, noise):
    _, _, seq_len, units = hidden.shape
    block = out_grad.shape[3]
    width = block * lax.axis_size("tensor")
    layers = lax.axis_size("layer")
    bound = float((seq_len * layers * units * lax.axis_size("tensor") * width / 64.0) ** 0.5)
    piece, half = block // RING, units // 2
    dma = pltpu.SemaphoreType.DMA
    result = pl.pallas_call(
        functools.partial(kernel, bound),
        out_shape=pltpu.VMEM((width, units), BF16),
        in_specs=[pl.BlockSpec(memory_space=pltpu.SMEM)] + [pl.BlockSpec(memory_space=pltpu.HBM)] * 3,
        out_specs=pl.BlockSpec(memory_space=pltpu.VMEM),
        scratch_shapes=[
            pltpu.VMEM((seq_len, units), BF16),
            pltpu.VMEM((width, seq_len), BF16),
            pltpu.VMEM((width, units), BF16),
            pltpu.VMEM((2, RING, piece, half), BF16),
            pltpu.VMEM((2, RING, piece, half), BF16),
            pltpu.VMEM((2, RING, piece, half), BF16),
            pltpu.VMEM((2, RING, piece, half), BF16),
            pltpu.VMEM((2, piece, half), BF16),
            pltpu.VMEM((2, piece, half), BF16),
            pltpu.VMEM((2, piece, half), BF16),
            pltpu.VMEM((piece, units), F32),
            pltpu.VMEM((2, piece, half), BF16),
            pltpu.VMEM((RING, piece, half), BF16),
            pltpu.VMEM((8, half), F32),
            pltpu.VMEM((2 * RING, 8, 128), F32),
            pltpu.VMEM((7, 8, 128), F32),
            dma((3,)), dma((2, 7)), dma((2, 7)),
            dma((2, RING)), dma((2, RING)), dma((2, RING)), dma((2, RING)), dma((2, RING)),
            dma((2,)), dma((2,)), dma((2,)), dma((2,)),
            dma, dma, dma, dma, dma, dma, dma, dma, dma,
            dma((2,)), dma((2, 3)), dma((2, RING)), dma((2, RING, 3)),
        ],
        compiler_params=pltpu.CompilerParams(
            collective_id=0, has_side_effects=True, vmem_limit_bytes=46 * 1024 * 1024
        ),
        cost_estimate=pl.CostEstimate(
            flops=2 * width * units * seq_len, bytes_accessed=30_000_000, transcendentals=0
        ),
    )(lengths, *(pltpu.with_memory_space_constraint(a, pltpu.HBM) for a in (out_grad[0, 0].T, hidden[0, 0], noise[0])))
    return result[None]


def solution(mesh):
    placed = (
        P("layer", "dp", None, "tensor"),
        P("layer", "dp", None, "tensor"),
        P("dp"),
        P("layer", "dp", "tensor"),
    )
    return jax.shard_map(
        on_device, mesh=mesh, in_specs=placed, out_specs=P("layer", None, "tensor"), check_vma=False
    )
```
